32 devices in a mesh: row: 8 (over y, x, core), col: 4 (over z).
Axes of the slice: x: 2, y: 2, z: 4, core: 2. Of those that a mesh axis runs over, the one named last changes fastest.
Arguments:
- waveform: bfloat16 [32, 1024, 8192], P(('row', 'col')), may hold values from -50 to 50, as said below
- valid_mask: int32 [32, 1024], P(('row', 'col')), may hold values 0 or 1
- band_starts: int32 [10], replicated, may hold values from 0 to 4080
- station_map: int32 [1024], replicated, may hold values from 0 to 1023, each once
Outputs:
- stacked: bfloat16 [2, 160, 1024, 1024], P(None, None, 'row', 'col')
The draws below stay inside these ranges and needn't reach their ends.
Inputs may be any that keep to these rules, and one draw needn't show every extreme that they name: `waveform`: entries are real samples whose per-trace scale varies from trace to trace. `band_starts`: each band's 16 bins lie below 4096. `station_map`: a permutation of the stations.
All inputs are finite; a program needn't handle non-finite values. No bound on the sum of `valid_mask` on one device may be relied on, other than what follows from the above.
Results may differ from the reference program's by a relative error of at most 0.0068.
Values may be sent and summed in bfloat16 or wider, within the bound.
A program may use at most 128 MiB of HBM per device.

```python
import math
import jax
import jax.numpy as jnp
from jax import lax

L = 8192
BINS = 16
NBAND = 10
STATIONS = 1024
F = 160
WINDOWS = 32


def draw_waveform(key, part):
    key = jax.random.fold_in(key, 5)
    base_key, scale_key = jax.random.split(key)
    shape = (WINDOWS, STATIONS, L)
    base = jnp.clip(jax.random.normal(base_key, shape, jnp.float32), -5.0, 5.0)
    scales = jnp.exp(jax.random.uniform(scale_key, (WINDOWS, STATIONS, 1), jnp.float32, 0.0, math.log(10.0)))
    return (base * scales).astype(jnp.bfloat16)


def touch_ends(entries, own_key, smallest, largest):
    spot = [jax.random.randint(jax.random.fold_in(own_key, axis), (), 0, length) for axis, length in enumerate(entries.shape)]
    widest = entries.shape.index(max(entries.shape))
    beside = spot[:widest] + [(spot[widest] + 1) % entries.shape[widest]] + spot[widest + 1:]
    return entries.at[tuple(spot)].set(smallest).at[tuple(beside)].set(largest)


def setup_inputs(seed: int = 0) -> dict:
    key_of = jax.random.split(jax.random.key(seed), 5)
    waveform = draw_waveform(jax.random.fold_in(key_of[4], 71), 0)
    valid_mask = touch_ends((jax.random.randint(key_of[1], (WINDOWS, STATIONS), 0, 4) < 3).astype(jnp.int32), jax.random.fold_in(key_of[1], 1), 0, 1)
    band_starts = touch_ends(jax.random.randint(key_of[2], (NBAND,), 0, L // 2 - BINS + 1), jax.random.fold_in(key_of[2], 1), 0, (L // 2 - BINS + 1) - 1).astype(jnp.int32)
    station_map = jax.random.permutation(key_of[3], STATIONS).astype(jnp.int32)
    return dict(waveform=waveform, valid_mask=valid_mask, band_starts=band_starts, station_map=station_map)


def make_table(band_starts, length, bin_count):
    frequency = (band_starts[:, None] + jnp.arange(bin_count, dtype=jnp.int32)[None, :]).reshape(-1).astype(jnp.int32)
    samples = jnp.arange(length, dtype=jnp.int32)
    phase_index = frequency[:, None] * samples[None, :] % length
    angles = phase_index.astype(jnp.float32) * jnp.float32(2.0 * math.pi / length)
    scaling = jnp.float32(length ** (-0.5))
    return (jnp.concatenate([jnp.cos(angles), -jnp.sin(angles)], axis=0) * scaling).astype(jnp.bfloat16)

def whiten(spectra, mask_rows, band_count):
    count, double_bins, stations = spectra.shape
    half = double_bins // 2
    real_part = spectra[:, :half]
    imag_part = spectra[:, half:]
    power_bins = real_part * real_part + imag_part * imag_part
    band_mean = power_bins.reshape(count, band_count, half // band_count, stations).mean(axis=2, keepdims=True)
    band_mean = jnp.broadcast_to(band_mean, (count, band_count, half // band_count, stations)).reshape(count, half, stations)
    factor = mask_rows[:, None, :].astype(jnp.float32) / jnp.sqrt(power_bins + band_mean + 0.1)
    return jnp.concatenate([real_part * factor, imag_part * factor], axis=1).astype(jnp.bfloat16)

def reference(waveform, valid_mask, band_starts, station_map):
    dft_table = make_table(band_starts, L, BINS)

    def per_window(inputs):
        wave_rows, mask_row = inputs
        spectra = jnp.dot(dft_table, wave_rows.T, preferred_element_type=jnp.float32)
        sum_squares = lax.optimization_barrier(jnp.sum(jnp.square(wave_rows.astype(jnp.float32)), axis=1))
        rms_value = jnp.sqrt(sum_squares / L + 1e-06)
        spectra = spectra / rms_value[None, :]
        return whiten(spectra[None], mask_row[None], NBAND)[0]
    whitened = lax.map(per_window, (waveform, valid_mask))
    grid_order = whitened[:, :, station_map]
    scaling = jnp.float32(float(WINDOWS) ** (-0.5))

    def one_bin(index):
        real_part = lax.dynamic_index_in_dim(grid_order, index, 1, keepdims=False)
        imag_part = lax.dynamic_index_in_dim(grid_order, index + F, 1, keepdims=False)
        real_out = jnp.dot(real_part.T, real_part, preferred_element_type=jnp.float32) + jnp.dot(imag_part.T, imag_part, preferred_element_type=jnp.float32)
        imag_out = jnp.dot(real_part.T, imag_part, preferred_element_type=jnp.float32) - jnp.dot(imag_part.T, real_part, preferred_element_type=jnp.float32)
        return (jnp.stack([real_out, imag_out], axis=0) * scaling).astype(jnp.bfloat16)
    per_bin = lax.map(one_bin, jnp.arange(F, dtype=jnp.int32))
    return jnp.transpose(per_bin, (1, 0, 2, 3))
```

```python
import functools
import math

import jax
import jax.numpy as jnp
from jax import lax
from jax.experimental import pallas as pl
from jax.experimental.pallas import tpu as pltpu
from jax.sharding import PartitionSpec as P

BINS = 16
CHUNK = 1024
MESH = pl.DeviceIdType.MESH


def phase_tables(band_starts, length):
    frequency = (band_starts[:, None] + jnp.arange(BINS, dtype=jnp.int32)[None, :]).reshape(-1)

    def parts(samples):
        phase = frequency[:, None] * samples[None, :] % length
        angles = phase.astype(jnp.float32) * jnp.float32(2.0 * math.pi / length)
        return jnp.cos(angles), jnp.sin(angles)

    fine = parts(jnp.arange(CHUNK, dtype=jnp.int32))
    coarse = parts(jnp.arange(128, dtype=jnp.int32) * CHUNK)
    scaling = jnp.float32(length ** (-0.5))
    return fine + (coarse[0] * scaling, coarse[1] * scaling)


def spectra_kernel(
    length, wave, fine_cos, fine_sin, coarse_cos, coarse_sin, mask, order, out, acc, squares, white
):
    step = pl.program_id(0)
    stations = wave.shape[1]
    double_bins = acc.shape[0]
    bands = double_bins // (2 * BINS)

    @pl.when(step == 0)
    def _():
        acc[...] = jnp.zeros_like(acc)
        squares[...] = jnp.zeros_like(squares)

    lane = lax.broadcasted_iota(jnp.int32, coarse_cos.shape, 1)
    first_cos = jnp.sum(jnp.where(lane == step, coarse_cos[...], 0.0), axis=1, keepdims=True)
    first_sin = jnp.sum(jnp.where(lane == step, coarse_sin[...], 0.0), axis=1, keepdims=True)
    real = (first_cos * fine_cos[...] - first_sin * fine_sin[...]).astype(jnp.bfloat16)
    imag = (-(first_sin * fine_cos[...]) - first_cos * fine_sin[...]).astype(jnp.bfloat16)
    table = jnp.concatenate(
        [real.reshape(bands, BINS, CHUNK), imag.reshape(bands, BINS, CHUNK)], axis=1
    ).reshape(double_bins, CHUNK)
    acc[...] += lax.dot_general(
        table, wave[0], (((1,), (1,)), ((), ())), preferred_element_type=jnp.float32
    )
    total = squares[...]
    for tile in range(CHUNK // 128):
        part = wave[0, :, tile * 128 : (tile + 1) * 128].astype(jnp.float32)
        total = total + part * part
    squares[...] = total

    @pl.when(step == pl.num_programs(0) - 1)
    def _():
        ones = jnp.ones((8, 128), jnp.float32)
        sums = lax.dot_general(
            ones,
            squares[...],
            (((1,), (1,)), ((), ())),
            precision=lax.Precision.HIGHEST,
            preferred_element_type=jnp.float32,
        )[0:1]
        inverse = 1.0 / jnp.sqrt(sums / length + 1e-06)
        valid = mask[...].astype(jnp.float32)
        for band in range(bands):
            top = band * 2 * BINS
            re = acc[top : top + BINS, :] * inverse
            im = acc[top + BINS : top + 2 * BINS, :] * inverse
            power = re * re + im * im
            mean = jnp.mean(power, axis=0, keepdims=True)
            factor = valid / jnp.sqrt(power + mean + 0.1)
            white[top : top + BINS, :] = (re * factor).astype(jnp.bfloat16)
            white[top + BINS : top + 2 * BINS, :] = (im * factor).astype(jnp.bfloat16)
        blocks, _, width = out.shape
        group = 256
        for start in range(0, stations, group):
            source = lax.broadcasted_iota(jnp.int32, (stations, group), 0)
            pick = (source == order[0:1, start : start + group]).astype(jnp.float32)
            placed = jnp.dot(
                white[...], pick.astype(jnp.bfloat16), preferred_element_type=jnp.float32
            ).astype(jnp.bfloat16)
            for inner in range(group // width):
                out[start // width + inner] = placed[:, inner * width : (inner + 1) * width]


def exchange_kernel(
    rows, cols, white, row_all, col_all,
    local_sem, row_sent, row_got, col_sent, col_got,
    right_sent, right_got, left_sent, left_got, chip_sent, chip_got, pair_sent, pair_got,
):
    r = lax.axis_index("row")
    c = lax.axis_index("col")
    chips = rows // 2
    core = lax.rem(r, 2)
    chip = r // 2
    twin = r + 1 - 2 * core
    per = rows // cols

    barrier = pltpu.get_barrier_semaphore()
    for d in range(1, rows):
        pl.semaphore_signal(
            barrier, inc=1, device_id=(lax.rem(r + d, rows), c), device_id_type=MESH
        )
    for d in range(1, cols):
        pl.semaphore_signal(
            barrier, inc=1, device_id=(r, lax.rem(c + d, cols)), device_id_type=MESH
        )
    pl.semaphore_wait(barrier, rows - 1 + cols - 1)

    def remote(src, dst, sent, got, target):
        return pltpu.make_async_remote_copy(
            src_ref=src, dst_ref=dst, send_sem=sent, recv_sem=got,
            device_id=target, device_id_type=MESH,
        )

    def col_part(block):
        return white.at[pl.ds(block * per, per)]

    col_first = []
    for d in range(1, cols):
        other = lax.rem(c + d, cols)
        col_first.append(
            remote(col_part(other), col_all.at[c, r], col_sent.at[d], col_got.at[d], (r, other))
        )
        col_first[-1].start()
    row_first = []
    for d in range(1, rows):
        other = lax.rem(r + d, rows)
        row_first.append(
            remote(white.at[other], row_all.at[c, r], row_sent.at[d], row_got.at[d], (other, c))
        )
        row_first[-1].start()
    own_row = pltpu.make_async_copy(white.at[r], row_all.at[c, r], local_sem.at[0])
    own_row.start()
    own_col = pltpu.make_async_copy(col_part(c), col_all.at[c, r], local_sem.at[1])
    own_col.start()

    for d in range(1, rows):
        other = lax.rem(r + rows - d, rows)
        remote(
            white.at[r], row_all.at[c, other], row_sent.at[d], row_got.at[d], (other, c)
        ).wait_recv()
    own_row.wait()

    def to_right(step):
        block = c - step
        return remote(
            row_all.at[block], row_all.at[block],
            right_sent.at[step], right_got.at[step], (r, c + 1),
        )

    def to_left(step):
        block = c + step
        return remote(
            row_all.at[block], row_all.at[block],
            left_sent.at[step], left_got.at[step], (r, c - 1),
        )

    def from_left(step):
        block = c - 1 - step
        return remote(
            row_all.at[block], row_all.at[block],
            right_sent.at[step], right_got.at[step], (r, c - 1),
        )

    def from_right(step):
        block = c + 1 + step
        return remote(
            row_all.at[block], row_all.at[block],
            left_sent.at[step], left_got.at[step], (r, c + 1),
        )

    def sends(step, act):
        @pl.when((c + 1 < cols) & (c - step >= 0))
        def _():
            act(to_right(step))

        @pl.when((c - 1 >= 0) & (c + step < cols))
        def _():
            act(to_left(step))

    def receives(step):
        @pl.when(c - 1 - step >= 0)
        def _():
            from_left(step).wait_recv()

        @pl.when(c + 1 + step < cols)
        def _():
            from_right(step).wait_recv()

    sends(0, lambda copy: copy.start())

    for d in range(1, cols):
        other = lax.rem(c + cols - d, cols)
        remote(
            col_part(c), col_all.at[other, r], col_sent.at[d], col_got.at[d], (r, other)
        ).wait_recv()
    own_col.wait()

    def to_chip(d):
        other = 2 * lax.rem(chip + d, chips) + core
        return remote(
            col_all.at[:, r], col_all.at[:, r], chip_sent.at[d], chip_got.at[d], (other, c)
        )

    def from_chip(d):
        other = 2 * lax.rem(chip + chips - d, chips) + core
        return remote(
            col_all.at[:, other], col_all.at[:, other],
            chip_sent.at[d], chip_got.at[d], (other, c),
        )

    def to_twin(d):
        source = 2 * lax.rem(chip + chips - d, chips) + core
        return remote(
            col_all.at[:, source], col_all.at[:, source],
            pair_sent.at[d], pair_got.at[d], (twin, c),
        )

    def from_twin(d):
        source = 2 * lax.rem(chip + chips - d, chips) + 1 - core
        return remote(
            col_all.at[:, source], col_all.at[:, source],
            pair_sent.at[d], pair_got.at[d], (twin, c),
        )

    for d in range(1, chips):
        to_chip(d).start()
    to_twin(0).start()

    for step in range(max(cols - 1, chips - 1)):
        if step < cols - 1:
            receives(step)
            if step + 1 < cols - 1:
                sends(step + 1, lambda copy: copy.start())
        if step + 1 < chips:
            from_chip(step + 1).wait_recv()
            to_twin(step + 1).start()
    for d in range(chips):
        from_twin(d).wait_recv()
    for copy in col_first + row_first:
        copy.wait_send()
    for step in range(cols - 1):
        sends(step, lambda copy: copy.wait_send())
    for d in range(1, chips):
        to_chip(d).wait_send()
    for d in range(chips):
        to_twin(d).wait_send()


def pairs_kernel(scaling, row_block, col_block, out, spread):
    windows, depth, width = row_block.shape
    per = col_block.shape[1]
    for window in range(windows):
        lines = pl.ds(window * depth, depth)
        spread[0, lines, 0:width] = row_block[window].astype(jnp.float32)
        for part in range(per):
            spread[1 + part, lines, 0:width] = col_block[window, part].astype(jnp.float32)

    def pick(plane, line):
        picked = spread[plane, pl.ds(line, windows, stride=depth), :]
        return picked[:, 0:width].astype(jnp.bfloat16)

    for bin_ in range(BINS):
        left = jnp.concatenate([pick(0, bin_), pick(0, BINS + bin_)], axis=0)
        real = jnp.concatenate([pick(1 + part, bin_) for part in range(per)], axis=1)
        imag = jnp.concatenate([pick(1 + part, BINS + bin_) for part in range(per)], axis=1)
        right = jnp.concatenate(
            [jnp.concatenate([real, imag], axis=0), jnp.concatenate([imag, -real], axis=0)], axis=1
        )
        both = lax.dot_general(
            left, right, (((0,), (0,)), ((), ())), preferred_element_type=jnp.float32
        ) * scaling
        wide = per * width
        out[0, bin_] = both[:, 0:wide].astype(jnp.bfloat16)
        out[1, bin_] = both[:, wide : 2 * wide].astype(jnp.bfloat16)


def body(rows, cols, waveform, valid_mask, band_starts, station_map):
    _, stations, length = waveform.shape
    bands = band_starts.shape[0]
    double_bins = 2 * BINS * bands
    half = double_bins // 2
    width = stations // rows
    per = rows // cols
    windows = rows * cols
    steps = length // CHUNK
    whole = lambda shape: pl.BlockSpec(shape, lambda i: (0,) * len(shape))
    tables = phase_tables(band_starts, length)
    white = pl.pallas_call(
        functools.partial(spectra_kernel, length),
        grid=(steps,),
        out_shape=jax.ShapeDtypeStruct((rows, double_bins, width), jnp.bfloat16),
        in_specs=[
            pl.BlockSpec((1, stations, CHUNK), lambda i: (0, 0, i)),
            whole((half, CHUNK)),
            whole((half, CHUNK)),
            whole((half, 128)),
            whole((half, 128)),
            whole((1, stations)),
            whole((1, stations)),
        ],
        out_specs=whole((rows, double_bins, width)),
        scratch_shapes=[
            pltpu.VMEM((double_bins, stations), jnp.float32),
            pltpu.VMEM((stations, 128), jnp.float32),
            pltpu.VMEM((double_bins, stations), jnp.bfloat16),
        ],
        compiler_params=pltpu.CompilerParams(vmem_limit_bytes=48 * 1024 * 1024),
        name="spectra",
    )(waveform, *tables, valid_mask, station_map[None, :])

    dma = pltpu.SemaphoreType.DMA
    chips = rows // 2
    row_all, col_all = pl.pallas_call(
        functools.partial(exchange_kernel, rows, cols),
        out_shape=[
            jax.ShapeDtypeStruct((cols, rows, double_bins, width), jnp.bfloat16),
            jax.ShapeDtypeStruct((cols, rows, per, double_bins, width), jnp.bfloat16),
        ],
        in_specs=[pl.BlockSpec(memory_space=pl.ANY)],
        out_specs=[pl.BlockSpec(memory_space=pl.ANY)] * 2,
        scratch_shapes=[dma((2,)), dma((rows,)), dma((rows,)), dma((cols,)), dma((cols,))]
        + [dma((cols,))] * 4
        + [dma((chips,))] * 4,
        compiler_params=pltpu.CompilerParams(collective_id=0, has_side_effects=True),
        name="exchange",
    )(white)
    row_all = row_all.reshape(windows, double_bins, width)
    col_all = col_all.reshape(windows, per, double_bins, width)

    depth = 2 * BINS
    return pl.pallas_call(
        functools.partial(pairs_kernel, float(windows) ** (-0.5)),
        grid=(bands,),
        out_shape=jax.ShapeDtypeStruct((2, half, width, per * width), jnp.bfloat16),
        in_specs=[
            pl.BlockSpec((windows, depth, width), lambda b: (0, b, 0)),
            pl.BlockSpec((windows, per, depth, width), lambda b: (0, 0, b, 0)),
        ],
        out_specs=pl.BlockSpec((2, BINS, width, per * width), lambda b: (0, b, 0, 0)),
        scratch_shapes=[pltpu.VMEM((1 + per, windows * depth, 128), jnp.float32)],
        compiler_params=pltpu.CompilerParams(vmem_limit_bytes=48 * 1024 * 1024),
        name="pairs",
    )(row_all, col_all)


def solution(mesh):
    placed = (P(("row", "col"), None, None), P(("row", "col"), None), P(), P())
    return jax.shard_map(
        functools.partial(body, mesh.shape["row"], mesh.shape["col"]),
        mesh=mesh, in_specs=placed, out_specs=P(None, None, "row", "col"), check_vma=False,
    )
```

```python
import functools
import math

import jax
import jax.numpy as jnp
from jax import lax
from jax.experimental import pallas as pl
from jax.experimental.pallas import tpu as pltpu
from jax.sharding import PartitionSpec as P

BINS = 16
CHUNK = 1024
PIECES = 2
VMEM_BYTES = 60 * 1024 * 1024
MESH = pl.DeviceIdType.MESH


def phase_tables(band_starts, length):
    frequency = (band_starts[:, None] + jnp.arange(BINS, dtype=jnp.int32)[None, :]).reshape(-1)
    samples = jnp.arange(128, dtype=jnp.int32)
    samples = jnp.stack([samples, samples * 128])
    phase = frequency[None, :, None] * samples[:, None, :] % length
    angles = phase.astype(jnp.float32) * jnp.float32(2.0 * math.pi / length)
    return jnp.cos(angles), jnp.sin(angles)


def spectra_kernel(
    length, wave, cosines, sines, mask, order, out, acc, squares, white, fine_cos, fine_sin
):
    step = pl.program_id(0)
    stations = wave.shape[1]
    double_bins = acc.shape[0]
    bands = double_bins // (2 * BINS)

    @pl.when(step == 0)
    def _():
        acc[...] = jnp.zeros_like(acc)
        squares[...] = jnp.zeros_like(squares)
        for tile in range(CHUNK // 128):
            tile_cos = cosines[1, :, tile : tile + 1]
            tile_sin = sines[1, :, tile : tile + 1]
            lanes = slice(tile * 128, (tile + 1) * 128)
            fine_cos[:, lanes] = tile_cos * cosines[0] - tile_sin * sines[0]
            fine_sin[:, lanes] = tile_sin * cosines[0] + tile_cos * sines[0]

    scale = length ** (-0.5)
    here = lax.broadcasted_iota(jnp.int32, cosines.shape[1:], 1) == step * (CHUNK // 128)
    first_cos = scale * jnp.sum(jnp.where(here, cosines[1], 0.0), axis=1, keepdims=True)
    first_sin = scale * jnp.sum(jnp.where(here, sines[1], 0.0), axis=1, keepdims=True)
    real = (first_cos * fine_cos[...] - first_sin * fine_sin[...]).astype(jnp.bfloat16)
    imag = (-(first_sin * fine_cos[...]) - first_cos * fine_sin[...]).astype(jnp.bfloat16)
    table = jnp.concatenate(
        [real.reshape(bands, BINS, CHUNK), imag.reshape(bands, BINS, CHUNK)], axis=1
    ).reshape(double_bins, CHUNK)
    acc[...] += lax.dot_general(
        table, wave[0], (((1,), (1,)), ((), ())), preferred_element_type=jnp.float32
    )
    for top in range(0, stations, 64):
        total = squares[top : top + 64, :]
        for tile in range(CHUNK // 128):
            part = wave[0, top : top + 64, tile * 128 : (tile + 1) * 128].astype(jnp.float32)
            total = total + part * part
        squares[top : top + 64, :] = total

    @pl.when(step == pl.num_programs(0) - 1)
    def _():
        ones = jnp.ones((8, 128), jnp.float32)
        sums = lax.dot_general(
            ones,
            squares[...],
            (((1,), (1,)), ((), ())),
            precision=lax.Precision.HIGHEST,
            preferred_element_type=jnp.float32,
        )[0:1]
        inverse = 1.0 / jnp.sqrt(sums / length + 1e-06)
        valid = mask[...].astype(jnp.float32)
        for band in range(bands):
            top = band * 2 * BINS
            re = acc[top : top + BINS, :] * inverse
            im = acc[top + BINS : top + 2 * BINS, :] * inverse
            power = re * re + im * im
            mean = jnp.mean(power, axis=0, keepdims=True)
            factor = valid / jnp.sqrt(power + mean + 0.1)
            white[top : top + BINS, :] = (re * factor).astype(jnp.bfloat16)
            white[top + BINS : top + 2 * BINS, :] = (im * factor).astype(jnp.bfloat16)
        blocks, _, width = out.shape
        group = 256
        for start in range(0, stations, group):
            source = lax.broadcasted_iota(jnp.int32, (stations, group), 0)
            pick = (source == order[0:1, start : start + group]).astype(jnp.float32)
            placed = jnp.dot(
                white[...], pick.astype(jnp.bfloat16), preferred_element_type=jnp.float32
            ).astype(jnp.bfloat16)
            for inner in range(group // width):
                out[start // width + inner] = placed[:, inner * width : (inner + 1) * width]


def exchange_kernel(
    rows, cols, white, row_all, col_all,
    local_sem, row_sent, row_got, col_sent, col_got,
    right_sent, right_got, left_sent, left_got, chip_sent, chip_got, pair_sent, pair_got,
):
    r = lax.axis_index("row")
    c = lax.axis_index("col")
    chips = rows // 2
    core = lax.rem(r, 2)
    chip = r // 2
    twin = r + 1 - 2 * core
    per = rows // cols

    barrier = pltpu.get_barrier_semaphore()
    for d in range(1, rows):
        pl.semaphore_signal(
            barrier, inc=1, device_id=(lax.rem(r + d, rows), c), device_id_type=MESH
        )
    for d in range(1, cols):
        pl.semaphore_signal(
            barrier, inc=1, device_id=(r, lax.rem(c + d, cols)), device_id_type=MESH
        )
    pl.semaphore_wait(barrier, rows - 1 + cols - 1)

    def remote(src, dst, sent, got, target):
        return pltpu.make_async_remote_copy(
            src_ref=src, dst_ref=dst, send_sem=sent, recv_sem=got,
            device_id=target, device_id_type=MESH,
        )

    def col_part(block):
        return white.at[pl.ds(block * per, per)]

    col_first = []
    for d in range(1, cols):
        other = lax.rem(c + d, cols)
        col_first.append(
            remote(col_part(other), col_all.at[c, r], col_sent.at[d], col_got.at[d], (r, other))
        )
        col_first[-1].start()
    row_first = []
    for d in range(1, rows):
        other = lax.rem(r + d, rows)
        row_first.append(
            remote(white.at[other], row_all.at[c, r], row_sent.at[d], row_got.at[d], (other, c))
        )
        row_first[-1].start()
    own_row = pltpu.make_async_copy(white.at[r], row_all.at[c, r], local_sem.at[0])
    own_row.start()
    own_col = pltpu.make_async_copy(col_part(c), col_all.at[c, r], local_sem.at[1])
    own_col.start()

    for d in range(1, rows):
        other = lax.rem(r + rows - d, rows)
        remote(
            white.at[r], row_all.at[c, other], row_sent.at[d], row_got.at[d], (other, c)
        ).wait_recv()
    own_row.wait()

    def piece_of(block, piece):
        return row_all.at[block, pl.ds(piece * (rows // PIECES), rows // PIECES)]

    def passing(block, piece, sent, got, step, target):
        ref = piece_of(block, piece)
        return remote(ref, ref, sent.at[step, piece], got.at[step, piece], (r, target))

    def sends(step, piece, act):
        @pl.when((c + 1 < cols) & (c - step >= 0))
        def _():
            act(passing(c - step, piece, right_sent, right_got, step, c + 1))

        @pl.when((c - 1 >= 0) & (c + step < cols))
        def _():
            act(passing(c + step, piece, left_sent, left_got, step, c - 1))

    def receives(step, piece):
        @pl.when(c - 1 - step >= 0)
        def _():
            passing(c - 1 - step, piece, right_sent, right_got, step, c - 1).wait_recv()

        @pl.when(c + 1 + step < cols)
        def _():
            passing(c + 1 + step, piece, left_sent, left_got, step, c + 1).wait_recv()

    for piece in range(PIECES):
        sends(0, piece, lambda copy: copy.start())

    for d in range(1, cols):
        other = lax.rem(c + cols - d, cols)
        remote(
            col_part(c), col_all.at[other, r], col_sent.at[d], col_got.at[d], (r, other)
        ).wait_recv()
    own_col.wait()

    def to_chip(d):
        other = 2 * lax.rem(chip + d, chips) + core
        return remote(
            col_all.at[:, r], col_all.at[:, r], chip_sent.at[d], chip_got.at[d], (other, c)
        )

    def from_chip(d):
        other = 2 * lax.rem(chip + chips - d, chips) + core
        return remote(
            col_all.at[:, other], col_all.at[:, other],
            chip_sent.at[d], chip_got.at[d], (other, c),
        )

    def to_twin(d):
        source = 2 * lax.rem(chip + chips - d, chips) + core
        return remote(
            col_all.at[:, source], col_all.at[:, source],
            pair_sent.at[d], pair_got.at[d], (twin, c),
        )

    def from_twin(d):
        source = 2 * lax.rem(chip + chips - d, chips) + 1 - core
        return remote(
            col_all.at[:, source], col_all.at[:, source],
            pair_sent.at[d], pair_got.at[d], (twin, c),
        )

    for d in range(1, chips):
        to_chip(d).start()
    to_twin(0).start()

    for step in range(cols - 2):
        for piece in range(PIECES):
            receives(step, piece)
            sends(step + 1, piece, lambda copy: copy.start())
    for d in range(1, chips):
        from_chip(d).wait_recv()
        to_twin(d).start()
    for piece in range(PIECES):
        receives(cols - 2, piece)
    for d in range(chips):
        from_twin(d).wait_recv()
    for copy in col_first + row_first:
        copy.wait_send()
    for step in range(cols - 1):
        for piece in range(PIECES):
            sends(step, piece, lambda copy: copy.wait_send())
    for d in range(1, chips):
        to_chip(d).wait_send()
    for d in range(chips):
        to_twin(d).wait_send()


def pairs_kernel(scaling, row_block, col_block, out):
    windows, _, width = row_block.shape
    per = col_block.shape[1]
    group = 16
    side = group * BINS
    into = lax.broadcasted_iota(jnp.int32, (side, side), 0)
    source = lax.broadcasted_iota(jnp.int32, (side, side), 1)
    swap = (into % group == source // BINS) & (into // group == source % BINS)
    swap = swap.astype(jnp.float32).astype(jnp.bfloat16)

    regrouped = []
    for part in range(2):
        bins = slice(part * BINS, (part + 1) * BINS)
        for first in range(0, windows, group):
            pieces = [row_block[first : first + group, bins, :].reshape(side, width)]
            for block in range(per):
                pieces.append(col_block[first : first + group, block, bins, :].reshape(side, width))
            regrouped.append(
                jnp.dot(
                    swap, jnp.concatenate(pieces, axis=1), preferred_element_type=jnp.float32
                ).astype(jnp.bfloat16)
            )
    half = len(regrouped) // 2
    wide = per * width
    for bin_ in range(BINS):
        lines = slice(bin_ * group, (bin_ + 1) * group)
        both = jnp.concatenate([block[lines] for block in regrouped], axis=0)
        swapped = jnp.concatenate(
            [block[lines, width:] for block in regrouped[half:]]
            + [-block[lines, width:] for block in regrouped[:half]],
            axis=0,
        )
        right = jnp.concatenate([both[:, width:], swapped], axis=1)
        result = lax.dot_general(
            both[:, 0:width], right, (((0,), (0,)), ((), ())), preferred_element_type=jnp.float32
        ) * scaling
        out[0, bin_] = result[:, 0:wide].astype(jnp.bfloat16)
        out[1, bin_] = result[:, wide : 2 * wide].astype(jnp.bfloat16)


def body(rows, cols, waveform, valid_mask, band_starts, station_map):
    _, stations, length = waveform.shape
    bands = band_starts.shape[0]
    double_bins = 2 * BINS * bands
    half = double_bins // 2
    width = stations // rows
    per = rows // cols
    windows = rows * cols
    steps = length // CHUNK
    whole = lambda shape: pl.BlockSpec(shape, lambda i: (0,) * len(shape))
    tables = phase_tables(band_starts, length)
    white = pl.pallas_call(
        functools.partial(spectra_kernel, length),
        grid=(steps,),
        out_shape=jax.ShapeDtypeStruct((rows, double_bins, width), jnp.bfloat16),
        in_specs=[
            pl.BlockSpec((1, stations, CHUNK), lambda i: (0, 0, i)),
            whole((2, half, 128)),
            whole((2, half, 128)),
            whole((1, stations)),
            whole((1, stations)),
        ],
        out_specs=whole((rows, double_bins, width)),
        scratch_shapes=[
            pltpu.VMEM((double_bins, stations), jnp.float32),
            pltpu.VMEM((stations, 128), jnp.float32),
            pltpu.VMEM((double_bins, stations), jnp.bfloat16),
            pltpu.VMEM((half, CHUNK), jnp.float32),
            pltpu.VMEM((half, CHUNK), jnp.float32),
        ],
        compiler_params=pltpu.CompilerParams(vmem_limit_bytes=VMEM_BYTES),
        name="spectra",
    )(waveform, *tables, valid_mask, station_map[None, :])

    dma = pltpu.SemaphoreType.DMA
    chips = rows // 2
    row_all, col_all = pl.pallas_call(
        functools.partial(exchange_kernel, rows, cols),
        out_shape=[
            jax.ShapeDtypeStruct((cols, rows, double_bins, width), jnp.bfloat16),
            jax.ShapeDtypeStruct((cols, rows, per, double_bins, width), jnp.bfloat16),
        ],
        in_specs=[pl.BlockSpec(memory_space=pl.ANY)],
        out_specs=[pl.BlockSpec(memory_space=pl.ANY)] * 2,
        scratch_shapes=[dma((2,)), dma((rows,)), dma((rows,)), dma((cols,)), dma((cols,))]
        + [dma((cols, PIECES))] * 4
        + [dma((chips,))] * 4,
        compiler_params=pltpu.CompilerParams(collective_id=0, has_side_effects=True, vmem_limit_bytes=VMEM_BYTES
        ),
        name="exchange",
    )(white)
    row_all = row_all.reshape(windows, double_bins, width)
    col_all = col_all.reshape(windows, per, double_bins, width)

    depth = 2 * BINS
    return pl.pallas_call(
        functools.partial(pairs_kernel, float(windows) ** (-0.5)),
        grid=(bands,),
        out_shape=jax.ShapeDtypeStruct((2, half, width, per * width), jnp.bfloat16),
        in_specs=[
            pl.BlockSpec((windows, depth, width), lambda b: (0, b, 0)),
            pl.BlockSpec((windows, per, depth, width), lambda b: (0, 0, b, 0)),
        ],
        out_specs=pl.BlockSpec((2, BINS, width, per * width), lambda b: (0, b, 0, 0)),
        compiler_params=pltpu.CompilerParams(vmem_limit_bytes=VMEM_BYTES),
        name="pairs",
    )(row_all, col_all)


def solution(mesh):
    placed = (P(("row", "col"), None, None), P(("row", "col"), None), P(), P())
    return jax.shard_map(
        functools.partial(body, mesh.shape["row"], mesh.shape["col"]),
        mesh=mesh, in_specs=placed, out_specs=P(None, None, "row", "col"), check_vma=False,
    )
```

```python
import functools
import math

import jax
import jax.numpy as jnp
from jax import lax
from jax.experimental import pallas as pl
from jax.experimental.pallas import tpu as pltpu
from jax.sharding import PartitionSpec as P

BINS = 16
CHUNK = 1024
PIECES = 2
VMEM_BYTES = 60 * 1024 * 1024
MESH = pl.DeviceIdType.MESH


def phase_tables(band_starts, length):
    frequency = (band_starts[:, None] + jnp.arange(BINS, dtype=jnp.int32)[None, :]).reshape(-1)
    samples = jnp.arange(128, dtype=jnp.int32)
    samples = jnp.stack([samples, samples * 128])
    phase = frequency[None, :, None] * samples[:, None, :] % length
    angles = phase.astype(jnp.float32) * jnp.float32(2.0 * math.pi / length)
    return jnp.cos(angles), jnp.sin(angles)


def spectra_kernel(
    length, wave, cosines, sines, mask, order, out, acc, squares, white, fine_cos, fine_sin
):
    step = pl.program_id(0)
    stations = wave.shape[1]
    double_bins = acc.shape[0]
    bands = double_bins // (2 * BINS)

    @pl.when(step == 0)
    def _():
        acc[...] = jnp.zeros_like(acc)
        squares[...] = jnp.zeros_like(squares)
        for tile in range(CHUNK // 128):
            tile_cos = cosines[1, :, tile : tile + 1]
            tile_sin = sines[1, :, tile : tile + 1]
            lanes = slice(tile * 128, (tile + 1) * 128)
            fine_cos[:, lanes] = tile_cos * cosines[0] - tile_sin * sines[0]
            fine_sin[:, lanes] = tile_sin * cosines[0] + tile_cos * sines[0]

    scale = length ** (-0.5)
    here = lax.broadcasted_iota(jnp.int32, cosines.shape[1:], 1) == step * (CHUNK // 128)
    first_cos = scale * jnp.sum(jnp.where(here, cosines[1], 0.0), axis=1, keepdims=True)
    first_sin = scale * jnp.sum(jnp.where(here, sines[1], 0.0), axis=1, keepdims=True)
    real = (first_cos * fine_cos[...] - first_sin * fine_sin[...]).astype(jnp.bfloat16)
    imag = (-(first_sin * fine_cos[...]) - first_cos * fine_sin[...]).astype(jnp.bfloat16)
    table = jnp.concatenate(
        [real.reshape(bands, BINS, CHUNK), imag.reshape(bands, BINS, CHUNK)], axis=1
    ).reshape(double_bins, CHUNK)
    acc[...] += lax.dot_general(
        table, wave[0], (((1,), (1,)), ((), ())), preferred_element_type=jnp.float32
    )
    for top in range(0, stations, 64):
        total = squares[top : top + 64, :]
        for tile in range(CHUNK // 128):
            part = wave[0, top : top + 64, tile * 128 : (tile + 1) * 128].astype(jnp.float32)
            total = total + part * part
        squares[top : top + 64, :] = total

    @pl.when(step == pl.num_programs(0) - 1)
    def _():
        ones = jnp.ones((8, 128), jnp.float32)
        sums = lax.dot_general(
            ones,
            squares[...],
            (((1,), (1,)), ((), ())),
            precision=lax.Precision.HIGHEST,
            preferred_element_type=jnp.float32,
        )[0:1]
        inverse = 1.0 / jnp.sqrt(sums / length + 1e-06)
        valid = mask[...].astype(jnp.float32)
        for band in range(bands):
            top = band * 2 * BINS
            re = acc[top : top + BINS, :] * inverse
            im = acc[top + BINS : top + 2 * BINS, :] * inverse
            power = re * re + im * im
            mean = jnp.mean(power, axis=0, keepdims=True)
            factor = valid / jnp.sqrt(power + mean + 0.1)
            white[top : top + BINS, :] = (re * factor).astype(jnp.bfloat16)
            white[top + BINS : top + 2 * BINS, :] = (im * factor).astype(jnp.bfloat16)
        blocks, _, width = out.shape
        group = 256
        for start in range(0, stations, group):
            source = lax.broadcasted_iota(jnp.int32, (stations, group), 0)
            pick = (source == order[0:1, start : start + group]).astype(jnp.float32)
            placed = jnp.dot(
                white[...], pick.astype(jnp.bfloat16), preferred_element_type=jnp.float32
            ).astype(jnp.bfloat16)
            for inner in range(group // width):
                out[start // width + inner] = placed[:, inner * width : (inner + 1) * width]


def exchange_kernel(
    rows, cols, white, row_all, col_all,
    local_sem, row_sent, row_got, col_sent, col_got,
    right_sent, right_got, left_sent, left_got, chip_sent, chip_got, pair_sent, pair_got,
):
    r = lax.axis_index("row")
    c = lax.axis_index("col")
    chips = rows // 2
    core = lax.rem(r, 2)
    chip = r // 2
    twin = r + 1 - 2 * core
    per = rows // cols

    barrier = pltpu.get_barrier_semaphore()
    for d in range(1, rows):
        pl.semaphore_signal(
            barrier, inc=1, device_id=(lax.rem(r + d, rows), c), device_id_type=MESH
        )
    for d in range(1, cols):
        pl.semaphore_signal(
            barrier, inc=1, device_id=(r, lax.rem(c + d, cols)), device_id_type=MESH
        )
    pl.semaphore_wait(barrier, rows - 1 + cols - 1)

    def remote(src, dst, sent, got, target):
        return pltpu.make_async_remote_copy(
            src_ref=src, dst_ref=dst, send_sem=sent, recv_sem=got,
            device_id=target, device_id_type=MESH,
        )

    def col_part(block):
        return white.at[pl.ds(block * per, per)]

    col_first = []
    for d in range(1, cols):
        other = lax.rem(c + d, cols)
        col_first.append(
            remote(col_part(other), col_all.at[c, r], col_sent.at[d], col_got.at[d], (r, other))
        )
        col_first[-1].start()
    row_first = []
    for d in range(1, rows):
        other = lax.rem(r + d, rows)
        row_first.append(
            remote(white.at[other], row_all.at[c, r], row_sent.at[d], row_got.at[d], (other, c))
        )
        row_first[-1].start()
    own_row = pltpu.make_async_copy(white.at[r], row_all.at[c, r], local_sem.at[0])
    own_row.start()
    own_col = pltpu.make_async_copy(col_part(c), col_all.at[c, r], local_sem.at[1])
    own_col.start()

    for d in range(1, rows):
        other = lax.rem(r + rows - d, rows)
        remote(
            white.at[r], row_all.at[c, other], row_sent.at[d], row_got.at[d], (other, c)
        ).wait_recv()
    own_row.wait()

    def piece_of(block, piece):
        return row_all.at[block, pl.ds(piece * (rows // PIECES), rows // PIECES)]

    def passing(block, piece, sent, got, step, target):
        ref = piece_of(block, piece)
        return remote(ref, ref, sent.at[step, piece], got.at[step, piece], (r, target))

    def sends(step, piece, act):
        @pl.when((c + 1 < cols) & (c - step >= 0))
        def _():
            act(passing(c - step, piece, right_sent, right_got, step, c + 1))

        @pl.when((c - 1 >= 0) & (c + step < cols))
        def _():
            act(passing(c + step, piece, left_sent, left_got, step, c - 1))

    def receives(step, piece):
        @pl.when(c - 1 - step >= 0)
        def _():
            passing(c - 1 - step, piece, right_sent, right_got, step, c - 1).wait_recv()

        @pl.when(c + 1 + step < cols)
        def _():
            passing(c + 1 + step, piece, left_sent, left_got, step, c + 1).wait_recv()

    for piece in range(PIECES):
        sends(0, piece, lambda copy: copy.start())

    for d in range(1, cols):
        other = lax.rem(c + cols - d, cols)
        remote(
            col_part(c), col_all.at[other, r], col_sent.at[d], col_got.at[d], (r, other)
        ).wait_recv()
    own_col.wait()

    def to_chip(d):
        other = 2 * lax.rem(chip + d, chips) + core
        return remote(
            col_all.at[:, r], col_all.at[:, r], chip_sent.at[d], chip_got.at[d], (other, c)
        )

    def from_chip(d):
        other = 2 * lax.rem(chip + chips - d, chips) + core
        return remote(
            col_all.at[:, other], col_all.at[:, other],
            chip_sent.at[d], chip_got.at[d], (other, c),
        )

    def to_twin(d):
        source = 2 * lax.rem(chip + chips - d, chips) + core
        return remote(
            col_all.at[:, source], col_all.at[:, source],
            pair_sent.at[d], pair_got.at[d], (twin, c),
        )

    def from_twin(d):
        source = 2 * lax.rem(chip + chips - d, chips) + 1 - core
        return remote(
            col_all.at[:, source], col_all.at[:, source],
            pair_sent.at[d], pair_got.at[d], (twin, c),
        )

    for d in range(1, chips):
        to_chip(d).start()
    to_twin(0).start()

    for step in range(cols - 2):
        for piece in range(PIECES):
            receives(step, piece)
            sends(step + 1, piece, lambda copy: copy.start())
    for d in range(1, chips):
        from_chip(d).wait_recv()
        to_twin(d).start()
    for piece in range(PIECES):
        receives(cols - 2, piece)
    for d in range(chips):
        from_twin(d).wait_recv()
    for copy in col_first + row_first:
        copy.wait_send()
    for step in range(cols - 1):
        for piece in range(PIECES):
            sends(step, piece, lambda copy: copy.wait_send())
    for d in range(1, chips):
        to_chip(d).wait_send()
    for d in range(chips):
        to_twin(d).wait_send()


def pairs_kernel(scaling, row_block, col_block, out):
    windows, _, width = row_block.shape
    per = col_block.shape[1]
    group = 16
    side = group * BINS
    into = lax.broadcasted_iota(jnp.int32, (side, side), 0)
    source = lax.broadcasted_iota(jnp.int32, (side, side), 1)
    swap = (into % group == source // BINS) & (into // group == source % BINS)
    swap = swap.astype(jnp.float32).astype(jnp.bfloat16)

    regrouped = []
    for part in range(2):
        bins = slice(part * BINS, (part + 1) * BINS)
        for first in range(0, windows, group):
            pieces = [row_block[first : first + group, bins, :].reshape(side, width)]
            for block in range(per):
                pieces.append(col_block[first : first + group, block, bins, :].reshape(side, width))
            regrouped.append(
                jnp.dot(
                    swap, jnp.concatenate(pieces, axis=1), preferred_element_type=jnp.float32
                ).astype(jnp.bfloat16)
            )
    half = len(regrouped) // 2
    wide = per * width
    together = max(1, 256 // (2 * windows))
    depth = together * 2 * windows
    owner = lax.broadcasted_iota(jnp.int32, (width, depth), 1) // (2 * windows)
    masks = [(owner == j).astype(jnp.float32).astype(jnp.bfloat16) for j in range(together)]
    for first in range(0, BINS, together):
        both, turned = [], []
        for bin_ in range(first, first + together):
            lines = slice(bin_ * group, (bin_ + 1) * group)
            both += [block[lines] for block in regrouped]
            turned += [-block[lines, 0:width] for block in regrouped[half:]]
            turned += [block[lines, 0:width] for block in regrouped[:half]]
        both = jnp.concatenate(both, axis=0)
        sides = [both[:, 0:width].T, jnp.concatenate(turned, axis=0).T]
        if together > 1:
            sides = [side * mask for mask in masks for side in sides]
        result = jnp.dot(
            jnp.concatenate(sides, axis=0), both[:, width:], preferred_element_type=jnp.float32
        )
        for j in range(together):
            for part in range(2):
                top = (2 * j + part) * width
                out[part, first + j] = (result[top : top + width] * scaling).astype(jnp.bfloat16)


def body(rows, cols, waveform, valid_mask, band_starts, station_map):
    _, stations, length = waveform.shape
    bands = band_starts.shape[0]
    double_bins = 2 * BINS * bands
    half = double_bins // 2
    width = stations // rows
    per = rows // cols
    windows = rows * cols
    steps = length // CHUNK
    whole = lambda shape: pl.BlockSpec(shape, lambda i: (0,) * len(shape))
    tables = phase_tables(band_starts, length)
    white = pl.pallas_call(
        functools.partial(spectra_kernel, length),
        grid=(steps,),
        out_shape=jax.ShapeDtypeStruct((rows, double_bins, width), jnp.bfloat16),
        in_specs=[
            pl.BlockSpec((1, stations, CHUNK), lambda i: (0, 0, i)),
            whole((2, half, 128)),
            whole((2, half, 128)),
            whole((1, stations)),
            whole((1, stations)),
        ],
        out_specs=whole((rows, double_bins, width)),
        scratch_shapes=[
            pltpu.VMEM((double_bins, stations), jnp.float32),
            pltpu.VMEM((stations, 128), jnp.float32),
            pltpu.VMEM((double_bins, stations), jnp.bfloat16),
            pltpu.VMEM((half, CHUNK), jnp.float32),
            pltpu.VMEM((half, CHUNK), jnp.float32),
        ],
        compiler_params=pltpu.CompilerParams(vmem_limit_bytes=VMEM_BYTES),
        name="spectra",
    )(waveform, *tables, valid_mask, station_map[None, :])

    dma = pltpu.SemaphoreType.DMA
    chips = rows // 2
    row_all, col_all = pl.pallas_call(
        functools.partial(exchange_kernel, rows, cols),
        out_shape=[
            jax.ShapeDtypeStruct((cols, rows, double_bins, width), jnp.bfloat16),
            jax.ShapeDtypeStruct((cols, rows, per, double_bins, width), jnp.bfloat16),
        ],
        in_specs=[pl.BlockSpec(memory_space=pl.ANY)],
        out_specs=[pl.BlockSpec(memory_space=pl.ANY)] * 2,
        scratch_shapes=[dma((2,)), dma((rows,)), dma((rows,)), dma((cols,)), dma((cols,))]
        + [dma((cols, PIECES))] * 4
        + [dma((chips,))] * 4,
        compiler_params=pltpu.CompilerParams(collective_id=0, has_side_effects=True, vmem_limit_bytes=VMEM_BYTES
        ),
        name="exchange",
    )(white)
    row_all = row_all.reshape(windows, double_bins, width)
    col_all = col_all.reshape(windows, per, double_bins, width)

    depth = 2 * BINS
    return pl.pallas_call(
        functools.partial(pairs_kernel, float(windows) ** (-0.5)),
        grid=(bands,),
        out_shape=jax.ShapeDtypeStruct((2, half, width, per * width), jnp.bfloat16),
        in_specs=[
            pl.BlockSpec((windows, depth, width), lambda b: (0, b, 0)),
            pl.BlockSpec((windows, per, depth, width), lambda b: (0, 0, b, 0)),
        ],
        out_specs=pl.BlockSpec((2, BINS, width, per * width), lambda b: (0, b, 0, 0)),
        compiler_params=pltpu.CompilerParams(vmem_limit_bytes=VMEM_BYTES),
        name="pairs",
    )(row_all, col_all)


def solution(mesh):
    placed = (P(("row", "col"), None, None), P(("row", "col"), None), P(), P())
    return jax.shard_map(
        functools.partial(body, mesh.shape["row"], mesh.shape["col"]),
        mesh=mesh, in_specs=placed, out_specs=P(None, None, "row", "col"), check_vma=False,
    )
```

```python
import functools
import math

import jax
import jax.numpy as jnp
from jax import lax
from jax.experimental import pallas as pl
from jax.experimental.pallas import tpu as pltpu
from jax.sharding import PartitionSpec as P

BINS = 16
CHUNK = 1024
PIECES = 2
VIEWS = 4
VMEM_BYTES = 60 * 1024 * 1024
MESH = pl.DeviceIdType.MESH


def phase_tables(band_starts, length):
    frequency = (band_starts[:, None] + jnp.arange(BINS, dtype=jnp.int32)[None, :]).reshape(-1)
    samples = jnp.arange(128, dtype=jnp.int32)
    samples = jnp.stack([samples, samples * 128])
    phase = frequency[None, :, None] * samples[:, None, :] % length
    angles = phase.astype(jnp.float32) * jnp.float32(2.0 * math.pi / length)
    return jnp.cos(angles), jnp.sin(angles)


def spectra_kernel(
    length, *refs
):
    waves, refs = refs[:VIEWS], refs[VIEWS:]
    cosines, sines, mask, order, out, acc, squares, white, fine_cos, fine_sin = refs
    step = pl.program_id(0)
    each = waves[0].shape[1]
    stations = each * VIEWS
    double_bins = acc.shape[0]
    bands = double_bins // (2 * BINS)

    @pl.when(step == 0)
    def _():
        acc[...] = jnp.zeros_like(acc)
        squares[...] = jnp.zeros_like(squares)
        for tile in range(CHUNK // 128):
            tile_cos = cosines[1, :, tile : tile + 1]
            tile_sin = sines[1, :, tile : tile + 1]
            lanes = slice(tile * 128, (tile + 1) * 128)
            fine_cos[:, lanes] = tile_cos * cosines[0] - tile_sin * sines[0]
            fine_sin[:, lanes] = tile_sin * cosines[0] + tile_cos * sines[0]

    scale = length ** (-0.5)
    here = lax.broadcasted_iota(jnp.int32, cosines.shape[1:], 1) == step * (CHUNK // 128)
    first_cos = scale * jnp.sum(jnp.where(here, cosines[1], 0.0), axis=1, keepdims=True)
    first_sin = scale * jnp.sum(jnp.where(here, sines[1], 0.0), axis=1, keepdims=True)
    real = (first_cos * fine_cos[...] - first_sin * fine_sin[...]).astype(jnp.bfloat16)
    imag = (-(first_sin * fine_cos[...]) - first_cos * fine_sin[...]).astype(jnp.bfloat16)
    table = jnp.concatenate(
        [real.reshape(bands, BINS, CHUNK), imag.reshape(bands, BINS, CHUNK)], axis=1
    ).reshape(double_bins, CHUNK)
    for view, wave in enumerate(waves):
        base = view * each
        acc[:, base : base + each] += lax.dot_general(
            table, wave[0], (((1,), (1,)), ((), ())), preferred_element_type=jnp.float32
        )
        for top in range(0, each, 64):
            total = squares[base + top : base + top + 64, :]
            for tile in range(CHUNK // 128):
                part = wave[0, top : top + 64, tile * 128 : (tile + 1) * 128].astype(jnp.float32)
                total = total + part * part
            squares[base + top : base + top + 64, :] = total

    @pl.when(step == pl.num_programs(0) - 1)
    def _():
        ones = jnp.ones((8, 128), jnp.float32)
        sums = lax.dot_general(
            ones,
            squares[...],
            (((1,), (1,)), ((), ())),
            precision=lax.Precision.HIGHEST,
            preferred_element_type=jnp.float32,
        )[0:1]
        inverse = 1.0 / jnp.sqrt(sums / length + 1e-06)
        valid = mask[...].astype(jnp.float32)
        for band in range(bands):
            top = band * 2 * BINS
            re = acc[top : top + BINS, :] * inverse
            im = acc[top + BINS : top + 2 * BINS, :] * inverse
            power = re * re + im * im
            mean = jnp.mean(power, axis=0, keepdims=True)
            factor = valid / jnp.sqrt(power + mean + 0.1)
            white[top : top + BINS, :] = (re * factor).astype(jnp.bfloat16)
            white[top + BINS : top + 2 * BINS, :] = (im * factor).astype(jnp.bfloat16)
        blocks, _, width = out.shape
        group = 256
        for start in range(0, stations, group):
            source = lax.broadcasted_iota(jnp.int32, (stations, group), 0)
            pick = (source == order[0:1, start : start + group]).astype(jnp.float32)
            placed = jnp.dot(
                white[...], pick.astype(jnp.bfloat16), preferred_element_type=jnp.float32
            ).astype(jnp.bfloat16)
            for inner in range(group // width):
                out[start // width + inner] = placed[:, inner * width : (inner + 1) * width]


def exchange_kernel(
    rows, cols, white, row_all, col_all,
    local_sem, row_sent, row_got, col_sent, col_got,
    right_sent, right_got, left_sent, left_got, chip_sent, chip_got, pair_sent, pair_got,
):
    r = lax.axis_index("row")
    c = lax.axis_index("col")
    chips = rows // 2
    core = lax.rem(r, 2)
    chip = r // 2
    twin = r + 1 - 2 * core
    per = rows // cols

    barrier = pltpu.get_barrier_semaphore()
    for d in range(1, rows):
        pl.semaphore_signal(
            barrier, inc=1, device_id=(lax.rem(r + d, rows), c), device_id_type=MESH
        )
    for d in range(1, cols):
        pl.semaphore_signal(
            barrier, inc=1, device_id=(r, lax.rem(c + d, cols)), device_id_type=MESH
        )
    pl.semaphore_wait(barrier, rows - 1 + cols - 1)

    def remote(src, dst, sent, got, target):
        return pltpu.make_async_remote_copy(
            src_ref=src, dst_ref=dst, send_sem=sent, recv_sem=got,
            device_id=target, device_id_type=MESH,
        )

    def col_part(block):
        return white.at[pl.ds(block * per, per)]

    col_first = []
    for d in range(1, cols):
        other = lax.rem(c + d, cols)
        col_first.append(
            remote(col_part(other), col_all.at[c, r], col_sent.at[d], col_got.at[d], (r, other))
        )
        col_first[-1].start()
    row_first = []
    for d in range(1, rows):
        other = lax.rem(r + d, rows)
        row_first.append(
            remote(white.at[other], row_all.at[c, r], row_sent.at[d], row_got.at[d], (other, c))
        )
        row_first[-1].start()
    own_row = pltpu.make_async_copy(white.at[r], row_all.at[c, r], local_sem.at[0])
    own_row.start()
    own_col = pltpu.make_async_copy(col_part(c), col_all.at[c, r], local_sem.at[1])
    own_col.start()

    for d in range(1, rows):
        other = lax.rem(r + rows - d, rows)
        remote(
            white.at[r], row_all.at[c, other], row_sent.at[d], row_got.at[d], (other, c)
        ).wait_recv()
    own_row.wait()

    def piece_of(block, piece):
        return row_all.at[block, pl.ds(piece * (rows // PIECES), rows // PIECES)]

    def passing(block, piece, sent, got, step, target):
        ref = piece_of(block, piece)
        return remote(ref, ref, sent.at[step, piece], got.at[step, piece], (r, target))

    def sends(step, piece, act):
        @pl.when((c + 1 < cols) & (c - step >= 0))
        def _():
            act(passing(c - step, piece, right_sent, right_got, step, c + 1))

        @pl.when((c - 1 >= 0) & (c + step < cols))
        def _():
            act(passing(c + step, piece, left_sent, left_got, step, c - 1))

    def receives(step, piece):
        @pl.when(c - 1 - step >= 0)
        def _():
            passing(c - 1 - step, piece, right_sent, right_got, step, c - 1).wait_recv()

        @pl.when(c + 1 + step < cols)
        def _():
            passing(c + 1 + step, piece, left_sent, left_got, step, c + 1).wait_recv()

    for piece in range(PIECES):
        sends(0, piece, lambda copy: copy.start())

    for d in range(1, cols):
        other = lax.rem(c + cols - d, cols)
        remote(
            col_part(c), col_all.at[other, r], col_sent.at[d], col_got.at[d], (r, other)
        ).wait_recv()
    own_col.wait()

    def to_chip(d):
        other = 2 * lax.rem(chip + d, chips) + core
        return remote(
            col_all.at[:, r], col_all.at[:, r], chip_sent.at[d], chip_got.at[d], (other, c)
        )

    def from_chip(d):
        other = 2 * lax.rem(chip + chips - d, chips) + core
        return remote(
            col_all.at[:, other], col_all.at[:, other],
            chip_sent.at[d], chip_got.at[d], (other, c),
        )

    def to_twin(d):
        source = 2 * lax.rem(chip + chips - d, chips) + core
        return remote(
            col_all.at[:, source], col_all.at[:, source],
            pair_sent.at[d], pair_got.at[d], (twin, c),
        )

    def from_twin(d):
        source = 2 * lax.rem(chip + chips - d, chips) + 1 - core
        return remote(
            col_all.at[:, source], col_all.at[:, source],
            pair_sent.at[d], pair_got.at[d], (twin, c),
        )

    for d in range(1, chips):
        to_chip(d).start()
    to_twin(0).start()

    for step in range(cols - 2):
        for piece in range(PIECES):
            receives(step, piece)
            sends(step + 1, piece, lambda copy: copy.start())
    for d in range(1, chips):
        from_chip(d).wait_recv()
        to_twin(d).start()
    for piece in range(PIECES):
        receives(cols - 2, piece)
    for d in range(chips):
        from_twin(d).wait_recv()
    for copy in col_first + row_first:
        copy.wait_send()
    for step in range(cols - 1):
        for piece in range(PIECES):
            sends(step, piece, lambda copy: copy.wait_send())
    for d in range(1, chips):
        to_chip(d).wait_send()
    for d in range(chips):
        to_twin(d).wait_send()


def pairs_kernel(scaling, row_block, col_block, out, held, sems):
    step = pl.program_id(0)
    last = pl.num_programs(0) - 1
    slot = lax.rem(step, 2)
    windows, _, width = row_block.shape
    per = col_block.shape[1]
    group = 16
    side = group * BINS
    into = lax.broadcasted_iota(jnp.int32, (side, side), 0)
    source = lax.broadcasted_iota(jnp.int32, (side, side), 1)
    swap = (into % group == source // BINS) & (into // group == source % BINS)
    swap = swap.astype(jnp.float32).astype(jnp.bfloat16)

    regrouped = []
    for part in range(2):
        bins = slice(part * BINS, (part + 1) * BINS)
        for first in range(0, windows, group):
            pieces = [row_block[first : first + group, bins, :].reshape(side, width)]
            for block in range(per):
                pieces.append(col_block[first : first + group, block, bins, :].reshape(side, width))
            regrouped.append(
                jnp.dot(
                    swap, jnp.concatenate(pieces, axis=1), preferred_element_type=jnp.float32
                ).astype(jnp.bfloat16)
            )
    half = len(regrouped) // 2
    wide = per * width
    together = max(1, 256 // (2 * windows))
    depth = together * 2 * windows
    owner = lax.broadcasted_iota(jnp.int32, (width, depth), 1) // (2 * windows)
    groups = BINS // together

    def copies(at_step, at_slot):
        return [
            pltpu.make_async_copy(
                held.at[at_slot, part, pl.ds(g * together, together)],
                out.at[part, pl.ds(at_step * BINS + g * together, together)],
                sems.at[at_slot, part, g],
            )
            for g in range(groups)
            for part in range(2)
        ]

    @pl.when(step >= 2)
    def _():
        for copy in copies(step - 2, slot):
            copy.wait()

    outgoing = copies(step, slot)
    masks = [(owner == j).astype(jnp.float32).astype(jnp.bfloat16) for j in range(together)]
    for first in range(0, BINS, together):
        both, turned = [], []
        for bin_ in range(first, first + together):
            lines = slice(bin_ * group, (bin_ + 1) * group)
            both += [block[lines] for block in regrouped]
            turned += [-block[lines, 0:width] for block in regrouped[half:]]
            turned += [block[lines, 0:width] for block in regrouped[:half]]
        both = jnp.concatenate(both, axis=0)
        sides = [both[:, 0:width].T, jnp.concatenate(turned, axis=0).T]
        if together > 1:
            sides = [side * mask for mask in masks for side in sides]
        result = jnp.dot(
            jnp.concatenate(sides, axis=0), both[:, width:], preferred_element_type=jnp.float32
        )
        for j in range(together):
            for part in range(2):
                top = (2 * j + part) * width
                held[slot, part, first + j] = (result[top : top + width] * scaling).astype(
                    jnp.bfloat16
                )
        for part in range(2):
            outgoing[first // together * 2 + part].start()

    @pl.when(step == last)
    def _():
        for copy in copies(step - 1, 1 - slot) + outgoing:
            copy.wait()


def body(rows, cols, waveform, valid_mask, band_starts, station_map):
    _, stations, length = waveform.shape
    bands = band_starts.shape[0]
    double_bins = 2 * BINS * bands
    half = double_bins // 2
    width = stations // rows
    per = rows // cols
    windows = rows * cols
    steps = length // CHUNK
    whole = lambda shape: pl.BlockSpec(shape, lambda i: (0,) * len(shape))
    tables = phase_tables(band_starts, length)
    white = pl.pallas_call(
        functools.partial(spectra_kernel, length),
        grid=(steps,),
        out_shape=jax.ShapeDtypeStruct((rows, double_bins, width), jnp.bfloat16),
        in_specs=[
            pl.BlockSpec((1, stations // VIEWS, CHUNK), lambda i, view=view: (0, view, i))
            for view in range(VIEWS)
        ]
        + [
            whole((2, half, 128)),
            whole((2, half, 128)),
            whole((1, stations)),
            whole((1, stations)),
        ],
        out_specs=whole((rows, double_bins, width)),
        scratch_shapes=[
            pltpu.VMEM((double_bins, stations), jnp.float32),
            pltpu.VMEM((stations, 128), jnp.float32),
            pltpu.VMEM((double_bins, stations), jnp.bfloat16),
            pltpu.VMEM((half, CHUNK), jnp.float32),
            pltpu.VMEM((half, CHUNK), jnp.float32),
        ],
        compiler_params=pltpu.CompilerParams(vmem_limit_bytes=VMEM_BYTES),
        name="spectra",
    )(*[waveform] * VIEWS, *tables, valid_mask, station_map[None, :])

    dma = pltpu.SemaphoreType.DMA
    chips = rows // 2
    row_all, col_all = pl.pallas_call(
        functools.partial(exchange_kernel, rows, cols),
        out_shape=[
            jax.ShapeDtypeStruct((cols, rows, double_bins, width), jnp.bfloat16),
            jax.ShapeDtypeStruct((cols, rows, per, double_bins, width), jnp.bfloat16),
        ],
        in_specs=[pl.BlockSpec(memory_space=pl.ANY)],
        out_specs=[pl.BlockSpec(memory_space=pl.ANY)] * 2,
        scratch_shapes=[dma((2,)), dma((rows,)), dma((rows,)), dma((cols,)), dma((cols,))]
        + [dma((cols, PIECES))] * 4
        + [dma((chips,))] * 4,
        compiler_params=pltpu.CompilerParams(collective_id=0, has_side_effects=True, vmem_limit_bytes=VMEM_BYTES
        ),
        name="exchange",
    )(white)
    row_all = row_all.reshape(windows, double_bins, width)
    col_all = col_all.reshape(windows, per, double_bins, width)

    depth = 2 * BINS
    return pl.pallas_call(
        functools.partial(pairs_kernel, float(windows) ** (-0.5)),
        grid=(bands,),
        out_shape=jax.ShapeDtypeStruct((2, half, width, per * width), jnp.bfloat16),
        in_specs=[
            pl.BlockSpec((windows, depth, width), lambda b: (0, b, 0)),
            pl.BlockSpec((windows, per, depth, width), lambda b: (0, 0, b, 0)),
        ],
        out_specs=pl.BlockSpec(memory_space=pl.ANY),
        scratch_shapes=[
            pltpu.VMEM((2, 2, BINS, width, per * width), jnp.bfloat16),
            pltpu.SemaphoreType.DMA((2, 2, BINS)),
        ],
        compiler_params=pltpu.CompilerParams(vmem_limit_bytes=VMEM_BYTES),
        name="pairs",
    )(row_all, col_all)


def solution(mesh):
    placed = (P(("row", "col"), None, None), P(("row", "col"), None), P(), P())
    return jax.shard_map(
        functools.partial(body, mesh.shape["row"], mesh.shape["col"]),
        mesh=mesh, in_specs=placed, out_specs=P(None, None, "row", "col"), check_vma=False,
    )
```

```python
import functools
import math

import jax
import jax.numpy as jnp
from jax import lax
from jax.experimental import pallas as pl
from jax.experimental.pallas import tpu as pltpu
from jax.sharding import PartitionSpec as P

BINS = 16
CHUNK = 1024
VMEM_BYTES = 60 * 1024 * 1024
MESH = pl.DeviceIdType.MESH


def phase_tables(band_starts, length):
    frequency = (band_starts[:, None] + jnp.arange(BINS, dtype=jnp.int32)[None, :]).reshape(-1)
    samples = jnp.arange(128, dtype=jnp.int32)
    samples = jnp.stack([samples, samples * 128])
    phase = frequency[None, :, None] * samples[:, None, :] % length
    angles = phase.astype(jnp.float32) * jnp.float32(2.0 * math.pi / length)
    return jnp.cos(angles), jnp.sin(angles)


def fill_fine(bins, cosines, sines, fine_cos, fine_sin):
    for tile in range(CHUNK // 128):
        tile_cos = cosines[1, bins, tile : tile + 1]
        tile_sin = sines[1, bins, tile : tile + 1]
        lanes = slice(tile * 128, (tile + 1) * 128)
        fine_cos[:, lanes] = tile_cos * cosines[0, bins] - tile_sin * sines[0, bins]
        fine_sin[:, lanes] = tile_sin * cosines[0, bins] + tile_cos * sines[0, bins]


def table_of(step, bins, length, cosines, sines, fine_cos, fine_sin):
    scale = length ** (-0.5)
    count = bins.stop - bins.start
    here = lax.broadcasted_iota(jnp.int32, (count, 128), 1) == step * (CHUNK // 128)
    first_cos = scale * jnp.sum(jnp.where(here, cosines[1, bins], 0.0), axis=1, keepdims=True)
    first_sin = scale * jnp.sum(jnp.where(here, sines[1, bins], 0.0), axis=1, keepdims=True)
    real = (first_cos * fine_cos[...] - first_sin * fine_sin[...]).astype(jnp.bfloat16)
    imag = (-(first_sin * fine_cos[...]) - first_cos * fine_sin[...]).astype(jnp.bfloat16)
    return jnp.concatenate(
        [real.reshape(-1, BINS, CHUNK), imag.reshape(-1, BINS, CHUNK)], axis=1
    ).reshape(2 * count, CHUNK)


def transform(table, wave):
    return lax.dot_general(
        table, wave, (((1,), (1,)), ((), ())), preferred_element_type=jnp.float32
    )


def whiten_and_place(acc, inverse, mask, order, white, out):
    stations = acc.shape[1]
    valid = mask[...].astype(jnp.float32)
    for top in range(0, acc.shape[0], 2 * BINS):
        re = acc[top : top + BINS, :] * inverse
        im = acc[top + BINS : top + 2 * BINS, :] * inverse
        power = re * re + im * im
        mean = jnp.mean(power, axis=0, keepdims=True)
        factor = valid / jnp.sqrt(power + mean + 0.1)
        white[top : top + BINS, :] = (re * factor).astype(jnp.bfloat16)
        white[top + BINS : top + 2 * BINS, :] = (im * factor).astype(jnp.bfloat16)
    width = out.shape[2]
    group = 256
    for start in range(0, stations, group):
        source = lax.broadcasted_iota(jnp.int32, (stations, group), 0)
        pick = (source == order[0:1, start : start + group]).astype(jnp.float32)
        placed = jnp.dot(
            white[...], pick.astype(jnp.bfloat16), preferred_element_type=jnp.float32
        ).astype(jnp.bfloat16)
        for inner in range(group // width):
            out[start // width + inner] = placed[:, inner * width : (inner + 1) * width]


def spectra_kernel(
    length, wave, cosines, sines, mask, order, out, inverse, acc, squares, white, fine_cos, fine_sin
):
    step = pl.program_id(0)
    stations = wave.shape[1]
    bins = slice(0, acc.shape[0] // 2)

    @pl.when(step == 0)
    def _():
        acc[...] = jnp.zeros_like(acc)
        squares[...] = jnp.zeros_like(squares)
        fill_fine(bins, cosines, sines, fine_cos, fine_sin)

    acc[...] += transform(
        table_of(step, bins, length, cosines, sines, fine_cos, fine_sin), wave[0]
    )
    for top in range(0, stations, 64):
        total = squares[top : top + 64, :]
        for tile in range(CHUNK // 128):
            part = wave[0, top : top + 64, tile * 128 : (tile + 1) * 128].astype(jnp.float32)
            total = total + part * part
        squares[top : top + 64, :] = total

    @pl.when(step == pl.num_programs(0) - 1)
    def _():
        ones = jnp.ones((8, 128), jnp.float32)
        sums = lax.dot_general(
            ones,
            squares[...],
            (((1,), (1,)), ((), ())),
            precision=lax.Precision.HIGHEST,
            preferred_element_type=jnp.float32,
        )[0:1]
        inverse[...] = 1.0 / jnp.sqrt(sums / length + 1e-06)
        whiten_and_place(acc, inverse[...], mask, order, white, out)


def exchange_kernel(
    rows, cols, ready, waveform, cosines, sines, mask, order, inverse, row_all, col_all,
    local_sem, row_sent, row_got, col_sent, col_got,
    right_sent, right_got, left_sent, left_got, chip_sent, chip_got, pair_sent, pair_got,
    waves, wave_sem, acc, white, fine_cos, fine_sin, later,
):
    r = lax.axis_index("row")
    c = lax.axis_index("col")
    chips = rows // 2
    core = lax.rem(r, 2)
    chip = r // 2
    twin = r + 1 - 2 * core
    per = rows // cols
    length = waveform.shape[2]
    steps = length // CHUNK
    sources = (ready, later)
    sizes = [source.shape[1] for source in sources]
    tops = (0, sizes[0])

    def fetch(step):
        slot = lax.rem(step, 2)
        return pltpu.make_async_copy(
            waveform.at[0, :, pl.ds(pl.multiple_of(step * CHUNK, CHUNK), CHUNK)],
            waves.at[slot],
            wave_sem.at[slot],
        )

    fetch(0).start()
    barrier = pltpu.get_barrier_semaphore()
    for d in range(1, rows):
        pl.semaphore_signal(
            barrier, inc=1, device_id=(lax.rem(r + d, rows), c), device_id_type=MESH
        )
    for d in range(1, cols):
        pl.semaphore_signal(
            barrier, inc=1, device_id=(r, lax.rem(c + d, cols)), device_id_type=MESH
        )
    pl.semaphore_wait(barrier, rows - 1 + cols - 1)

    def remote(src, dst, sent, got, target):
        return pltpu.make_async_remote_copy(
            src_ref=src, dst_ref=dst, send_sem=sent, recv_sem=got,
            device_id=target, device_id_type=MESH,
        )

    def lines(half):
        return pl.ds(tops[half], sizes[half])

    def col_part(half, block):
        return sources[half].at[pl.ds(block * per, per)]

    def col_first(half, d):
        other = lax.rem(c + d, cols)
        return remote(
            col_part(half, other), col_all.at[c, r, :, lines(half)],
            col_sent.at[half, d], col_got.at[half, d], (r, other),
        )

    def row_first(half, d):
        other = lax.rem(r + d, rows)
        return remote(
            sources[half].at[other], row_all.at[c, r, lines(half)],
            row_sent.at[half, d], row_got.at[half, d], (other, c),
        )

    def own_row(half):
        return pltpu.make_async_copy(
            sources[half].at[r], row_all.at[c, r, lines(half)], local_sem.at[half, 0]
        )

    def own_col(half):
        return pltpu.make_async_copy(
            col_part(half, c), col_all.at[c, r, :, lines(half)], local_sem.at[half, 1]
        )

    def start_firsts(half):
        for d in range(1, cols):
            col_first(half, d).start()
        for d in range(1, rows):
            row_first(half, d).start()
        own_row(half).start()
        own_col(half).start()

    def passing(block, half, sent, got, step, target):
        ref = row_all.at[block, :, lines(half)]
        return remote(ref, ref, sent.at[step, half], got.at[step, half], (r, target))

    def sends(step, half, act):
        @pl.when((c + 1 < cols) & (c - step >= 0))
        def _():
            act(passing(c - step, half, right_sent, right_got, step, c + 1))

        @pl.when((c - 1 >= 0) & (c + step < cols))
        def _():
            act(passing(c + step, half, left_sent, left_got, step, c - 1))

    def receives(step, half):
        @pl.when(c - 1 - step >= 0)
        def _():
            passing(c - 1 - step, half, right_sent, right_got, step, c - 1).wait_recv()

        @pl.when(c + 1 + step < cols)
        def _():
            passing(c + 1 + step, half, left_sent, left_got, step, c + 1).wait_recv()

    def moving(half, source, sent, got, d, target):
        ref = col_all.at[:, source, :, lines(half)]
        return remote(ref, ref, sent.at[half, d], got.at[half, d], (target, c))

    def to_chip(half, d):
        other = 2 * lax.rem(chip + d, chips) + core
        return moving(half, r, chip_sent, chip_got, d, other)

    def from_chip(half, d):
        other = 2 * lax.rem(chip + chips - d, chips) + core
        return moving(half, other, chip_sent, chip_got, d, other)

    def to_twin(half, d):
        source = 2 * lax.rem(chip + chips - d, chips) + core
        return moving(half, source, pair_sent, pair_got, d, twin)

    def from_twin(half, d):
        source = 2 * lax.rem(chip + chips - d, chips) + 1 - core
        return moving(half, source, pair_sent, pair_got, d, twin)

    def start_seconds(half):
        for d in range(1, rows):
            other = lax.rem(r + rows - d, rows)
            remote(
                sources[half].at[r], row_all.at[c, other, lines(half)],
                row_sent.at[half, d], row_got.at[half, d], (other, c),
            ).wait_recv()
        own_row(half).wait()
        sends(0, half, lambda copy: copy.start())
        for d in range(1, cols):
            other = lax.rem(c + cols - d, cols)
            remote(
                col_part(half, c), col_all.at[other, r, :, lines(half)],
                col_sent.at[half, d], col_got.at[half, d], (r, other),
            ).wait_recv()
        own_col(half).wait()
        for d in range(1, chips):
            to_chip(half, d).start()
        to_twin(half, 0).start()

    start_firsts(0)

    bins = slice(sizes[0] // 2, sum(sizes) // 2)
    acc[...] = jnp.zeros_like(acc)
    fill_fine(bins, cosines, sines, fine_cos, fine_sin)

    def chunk(step, carry):
        @pl.when(step + 1 < steps)
        def _():
            fetch(step + 1).start()

        fetch(step).wait()
        acc[...] += transform(
            table_of(step, bins, length, cosines, sines, fine_cos, fine_sin),
            waves[lax.rem(step, 2)],
        )
        return carry

    pause = max(1, steps * 3 // 4)
    lax.fori_loop(0, pause, chunk, 0)
    start_seconds(0)
    lax.fori_loop(pause, steps, chunk, 0)
    whiten_and_place(acc, inverse[...], mask, order, white, later)
    start_firsts(1)
    start_seconds(1)

    for step in range(cols - 2):
        for half in range(2):
            receives(step, half)
            sends(step + 1, half, lambda copy: copy.start())
    for half in range(2):
        for d in range(1, chips):
            from_chip(half, d).wait_recv()
            to_twin(half, d).start()
    for half in range(2):
        receives(cols - 2, half)
    for half in range(2):
        for d in range(chips):
            from_twin(half, d).wait_recv()
            to_twin(half, d).wait_send()
        for d in range(1, cols):
            col_first(half, d).wait_send()
        for d in range(1, rows):
            row_first(half, d).wait_send()
        for step in range(cols - 1):
            sends(step, half, lambda copy: copy.wait_send())
        for d in range(1, chips):
            to_chip(half, d).wait_send()


def pairs_kernel(scaling, row_block, col_block, out, held, sems):
    step = pl.program_id(0)
    last = pl.num_programs(0) - 1
    slot = lax.rem(step, 2)
    windows, _, width = row_block.shape
    per = col_block.shape[1]
    group = 16
    side = group * BINS
    into = lax.broadcasted_iota(jnp.int32, (side, side), 0)
    source = lax.broadcasted_iota(jnp.int32, (side, side), 1)
    swap = (into % group == source // BINS) & (into // group == source % BINS)
    swap = swap.astype(jnp.float32).astype(jnp.bfloat16)

    regrouped = []
    for part in range(2):
        bins = slice(part * BINS, (part + 1) * BINS)
        for first in range(0, windows, group):
            pieces = [row_block[first : first + group, bins, :].reshape(side, width)]
            for block in range(per):
                pieces.append(col_block[first : first + group, block, bins, :].reshape(side, width))
            regrouped.append(
                jnp.dot(
                    swap, jnp.concatenate(pieces, axis=1), preferred_element_type=jnp.float32
                ).astype(jnp.bfloat16)
            )
    half = len(regrouped) // 2
    wide = per * width
    together = max(1, 256 // (2 * windows))
    depth = together * 2 * windows
    owner = lax.broadcasted_iota(jnp.int32, (width, depth), 1) // (2 * windows)
    groups = BINS // together

    def copies(at_step, at_slot):
        return [
            pltpu.make_async_copy(
                held.at[at_slot, part, pl.ds(g * together, together)],
                out.at[part, pl.ds(at_step * BINS + g * together, together)],
                sems.at[at_slot, part, g],
            )
            for g in range(groups)
            for part in range(2)
        ]

    @pl.when(step >= 2)
    def _():
        for copy in copies(step - 2, slot):
            copy.wait()

    outgoing = copies(step, slot)
    masks = [(owner == j).astype(jnp.float32).astype(jnp.bfloat16) for j in range(together)]
    for first in range(0, BINS, together):
        both, turned = [], []
        for bin_ in range(first, first + together):
            lines = slice(bin_ * group, (bin_ + 1) * group)
            both += [block[lines] for block in regrouped]
            turned += [-block[lines, 0:width] for block in regrouped[half:]]
            turned += [block[lines, 0:width] for block in regrouped[:half]]
        both = jnp.concatenate(both, axis=0)
        sides = [both[:, 0:width].T, jnp.concatenate(turned, axis=0).T]
        if together > 1:
            sides = [side * mask for mask in masks for side in sides]
        result = jnp.dot(
            jnp.concatenate(sides, axis=0), both[:, width:], preferred_element_type=jnp.float32
        )
        for j in range(together):
            for part in range(2):
                top = (2 * j + part) * width
                held[slot, part, first + j] = (result[top : top + width] * scaling).astype(
                    jnp.bfloat16
                )
        for part in range(2):
            outgoing[first // together * 2 + part].start()

    @pl.when(step == last)
    def _():
        for copy in copies(step - 1, 1 - slot) + outgoing:
            copy.wait()


def body(rows, cols, waveform, valid_mask, band_starts, station_map):
    _, stations, length = waveform.shape
    bands = band_starts.shape[0]
    double_bins = 2 * BINS * bands
    half = double_bins // 2
    width = stations // rows
    per = rows // cols
    windows = rows * cols
    steps = length // CHUNK
    whole = lambda shape: pl.BlockSpec(shape, lambda i: (0,) * len(shape))
    tables = phase_tables(band_starts, length)
    order = station_map[None, :]
    sizes = (bands // 2 * 2 * BINS, (bands - bands // 2) * 2 * BINS)

    def work(size):
        return [
            pltpu.VMEM((size, stations), jnp.float32),
            pltpu.VMEM((size, stations), jnp.bfloat16),
            pltpu.VMEM((size // 2, CHUNK), jnp.float32),
            pltpu.VMEM((size // 2, CHUNK), jnp.float32),
        ]

    first = work(sizes[0])
    ready, inverse = pl.pallas_call(
        functools.partial(spectra_kernel, length),
        grid=(steps,),
        out_shape=[
            jax.ShapeDtypeStruct((rows, sizes[0], width), jnp.bfloat16),
            jax.ShapeDtypeStruct((1, stations), jnp.float32),
        ],
        in_specs=[
            pl.BlockSpec((1, stations, CHUNK), lambda i: (0, 0, i)),
            whole((2, half, 128)),
            whole((2, half, 128)),
            whole((1, stations)),
            whole((1, stations)),
        ],
        out_specs=[whole((rows, sizes[0], width)), whole((1, stations))],
        scratch_shapes=first[:1] + [pltpu.VMEM((stations, 128), jnp.float32)] + first[1:],
        compiler_params=pltpu.CompilerParams(vmem_limit_bytes=VMEM_BYTES),
        name="spectra",
    )(waveform, *tables, valid_mask, order)

    dma = pltpu.SemaphoreType.DMA
    chips = rows // 2
    in_vmem = pl.BlockSpec(memory_space=pltpu.VMEM)
    anywhere = pl.BlockSpec(memory_space=pl.ANY)
    row_all, col_all = pl.pallas_call(
        functools.partial(exchange_kernel, rows, cols),
        out_shape=[
            jax.ShapeDtypeStruct((cols, rows, double_bins, width), jnp.bfloat16),
            jax.ShapeDtypeStruct((cols, rows, per, double_bins, width), jnp.bfloat16),
        ],
        in_specs=[anywhere, anywhere] + [in_vmem] * 5,
        out_specs=[anywhere] * 2,
        scratch_shapes=[dma((2, 2))]
        + [dma((2, rows))] * 2
        + [dma((2, cols))] * 2
        + [dma((cols, 2))] * 4
        + [dma((2, chips))] * 4
        + [pltpu.VMEM((2, stations, CHUNK), jnp.bfloat16), dma((2,))]
        + work(sizes[1])
        + [pltpu.VMEM((rows, sizes[1], width), jnp.bfloat16)],
        compiler_params=pltpu.CompilerParams(
            collective_id=0, has_side_effects=True, vmem_limit_bytes=VMEM_BYTES
        ),
        name="exchange",
    )(ready, waveform, *tables, valid_mask, order, inverse)
    row_all = row_all.reshape(windows, double_bins, width)
    col_all = col_all.reshape(windows, per, double_bins, width)

    depth = 2 * BINS
    return pl.pallas_call(
        functools.partial(pairs_kernel, float(windows) ** (-0.5)),
        grid=(bands,),
        out_shape=jax.ShapeDtypeStruct((2, half, width, per * width), jnp.bfloat16),
        in_specs=[
            pl.BlockSpec((windows, depth, width), lambda b: (0, b, 0)),
            pl.BlockSpec((windows, per, depth, width), lambda b: (0, 0, b, 0)),
        ],
        out_specs=pl.BlockSpec(memory_space=pl.ANY),
        scratch_shapes=[
            pltpu.VMEM((2, 2, BINS, width, per * width), jnp.bfloat16),
            pltpu.SemaphoreType.DMA((2, 2, BINS)),
        ],
        compiler_params=pltpu.CompilerParams(vmem_limit_bytes=VMEM_BYTES),
        name="pairs",
    )(row_all, col_all)


def solution(mesh):
    placed = (P(("row", "col"), None, None), P(("row", "col"), None), P(), P())
    return jax.shard_map(
        functools.partial(body, mesh.shape["row"], mesh.shape["col"]),
        mesh=mesh, in_specs=placed, out_specs=P(None, None, "row", "col"), check_vma=False,
    )
```

```python
import functools
import math

import jax
import jax.numpy as jnp
from jax import lax
from jax.experimental import pallas as pl
from jax.experimental.pallas import tpu as pltpu
from jax.sharding import PartitionSpec as P

BINS = 16
CHUNK = 1024
PIECES = 2
VIEWS = 4
GROUP = 16
VMEM_BYTES = 60 * 1024 * 1024
MESH = pl.DeviceIdType.MESH


def phase_tables(band_starts, length):
    frequency = (band_starts[:, None] + jnp.arange(BINS, dtype=jnp.int32)[None, :]).reshape(-1)
    samples = jnp.arange(128, dtype=jnp.int32)
    samples = jnp.stack([samples, samples * 128])
    phase = frequency[None, :, None] * samples[:, None, :] % length
    angles = phase.astype(jnp.float32) * jnp.float32(2.0 * math.pi / length)
    return jnp.cos(angles), jnp.sin(angles)


def spectra_kernel(
    length, *refs
):
    waves, refs = refs[:VIEWS], refs[VIEWS:]
    cosines, sines, mask, order, out, sums_of, acc, squares, white, fine_cos, fine_sin = refs
    step = pl.program_id(0)
    each = waves[0].shape[1]
    stations = each * VIEWS
    double_bins = acc.shape[0]
    padding = sums_of.shape[1] - double_bins
    bands = double_bins // (2 * BINS)

    @pl.when(step == 0)
    def _():
        sums_of[...] = jnp.zeros_like(sums_of)
        squares[...] = jnp.zeros_like(squares)
        for tile in range(CHUNK // 128):
            tile_cos = cosines[1, :, tile : tile + 1]
            tile_sin = sines[1, :, tile : tile + 1]
            lanes = slice(tile * 128, (tile + 1) * 128)
            fine_cos[:, lanes] = tile_cos * cosines[0] - tile_sin * sines[0]
            fine_sin[:, lanes] = tile_sin * cosines[0] + tile_cos * sines[0]

    scale = length ** (-0.5)
    here = lax.broadcasted_iota(jnp.int32, cosines.shape[1:], 1) == step * (CHUNK // 128)
    first_cos = scale * jnp.sum(jnp.where(here, cosines[1], 0.0), axis=1, keepdims=True)
    first_sin = scale * jnp.sum(jnp.where(here, sines[1], 0.0), axis=1, keepdims=True)
    real = (first_cos * fine_cos[...] - first_sin * fine_sin[...]).astype(jnp.bfloat16)
    imag = (-(first_sin * fine_cos[...]) - first_cos * fine_sin[...]).astype(jnp.bfloat16)
    table = jnp.concatenate(
        [real.reshape(bands, BINS, CHUNK), imag.reshape(bands, BINS, CHUNK)], axis=1
    ).reshape(double_bins, CHUNK)
    table = jnp.concatenate([table, jnp.zeros((padding, CHUNK), jnp.bfloat16)], axis=0)
    for view, wave in enumerate(waves):
        base = view * each
        sums_of[base : base + each, :] += lax.dot_general(
            wave[0], table, (((1,), (1,)), ((), ())), preferred_element_type=jnp.float32
        )
        for top in range(0, each, 64):
            total = squares[base + top : base + top + 64, :]
            for tile in range(CHUNK // 128):
                part = wave[0, top : top + 64, tile * 128 : (tile + 1) * 128].astype(jnp.float32)
                total = total + part * part
            squares[base + top : base + top + 64, :] = total

    @pl.when(step == pl.num_programs(0) - 1)
    def _():
        acc[...] = sums_of[...].T[0:double_bins]
        ones = jnp.ones((8, 128), jnp.float32)
        sums = lax.dot_general(
            ones,
            squares[...],
            (((1,), (1,)), ((), ())),
            precision=lax.Precision.HIGHEST,
            preferred_element_type=jnp.float32,
        )[0:1]
        inverse = 1.0 / jnp.sqrt(sums / length + 1e-06)
        valid = mask[...].astype(jnp.float32)
        for band in range(bands):
            top = band * 2 * BINS
            re = acc[top : top + BINS, :] * inverse
            im = acc[top + BINS : top + 2 * BINS, :] * inverse
            power = re * re + im * im
            mean = jnp.mean(power, axis=0, keepdims=True)
            factor = valid / jnp.sqrt(power + mean + 0.1)
            white[top : top + BINS, :] = (re * factor).astype(jnp.bfloat16)
            white[top + BINS : top + 2 * BINS, :] = (im * factor).astype(jnp.bfloat16)
        blocks, _, width = out.shape
        group = 256
        for start in range(0, stations, group):
            source = lax.broadcasted_iota(jnp.int32, (stations, group), 0)
            pick = (source == order[0:1, start : start + group]).astype(jnp.float32)
            placed = jnp.dot(
                white[...], pick.astype(jnp.bfloat16), preferred_element_type=jnp.float32
            ).astype(jnp.bfloat16)
            for inner in range(group // width):
                out[start // width + inner] = placed[:, inner * width : (inner + 1) * width]


def exchange_kernel(
    rows, cols, white, row_all, col_all,
    local_sem, row_sent, row_got, col_sent, col_got,
    right_sent, right_got, left_sent, left_got, chip_sent, chip_got, pair_sent, pair_got,
):
    r = lax.axis_index("row")
    c = lax.axis_index("col")
    chips = rows // 2
    core = lax.rem(r, 2)
    chip = r // 2
    twin = r + 1 - 2 * core
    per = rows // cols

    barrier = pltpu.get_barrier_semaphore()
    for d in range(1, rows):
        pl.semaphore_signal(
            barrier, inc=1, device_id=(lax.rem(r + d, rows), c), device_id_type=MESH
        )
    for d in range(1, cols):
        pl.semaphore_signal(
            barrier, inc=1, device_id=(r, lax.rem(c + d, cols)), device_id_type=MESH
        )
    pl.semaphore_wait(barrier, rows - 1 + cols - 1)

    def remote(src, dst, sent, got, target):
        return pltpu.make_async_remote_copy(
            src_ref=src, dst_ref=dst, send_sem=sent, recv_sem=got,
            device_id=target, device_id_type=MESH,
        )

    def col_part(block):
        return white.at[pl.ds(block * per, per)]

    col_first = []
    for d in range(1, cols):
        other = lax.rem(c + d, cols)
        col_first.append(
            remote(col_part(other), col_all.at[c, r], col_sent.at[d], col_got.at[d], (r, other))
        )
        col_first[-1].start()
    row_first = []
    for d in range(1, rows):
        other = lax.rem(r + d, rows)
        row_first.append(
            remote(white.at[other], row_all.at[c, r], row_sent.at[d], row_got.at[d], (other, c))
        )
        row_first[-1].start()
    own_row = pltpu.make_async_copy(white.at[r], row_all.at[c, r], local_sem.at[0])
    own_row.start()
    own_col = pltpu.make_async_copy(col_part(c), col_all.at[c, r], local_sem.at[1])
    own_col.start()

    for d in range(1, rows):
        other = lax.rem(r + rows - d, rows)
        remote(
            white.at[r], row_all.at[c, other], row_sent.at[d], row_got.at[d], (other, c)
        ).wait_recv()
    own_row.wait()

    def piece_of(block, piece):
        return row_all.at[block, pl.ds(piece * (rows // PIECES), rows // PIECES)]

    def passing(block, piece, sent, got, step, target):
        ref = piece_of(block, piece)
        return remote(ref, ref, sent.at[step, piece], got.at[step, piece], (r, target))

    def sends(step, piece, act):
        @pl.when((c + 1 < cols) & (c - step >= 0))
        def _():
            act(passing(c - step, piece, right_sent, right_got, step, c + 1))

        @pl.when((c - 1 >= 0) & (c + step < cols))
        def _():
            act(passing(c + step, piece, left_sent, left_got, step, c - 1))

    def receives(step, piece):
        @pl.when(c - 1 - step >= 0)
        def _():
            passing(c - 1 - step, piece, right_sent, right_got, step, c - 1).wait_recv()

        @pl.when(c + 1 + step < cols)
        def _():
            passing(c + 1 + step, piece, left_sent, left_got, step, c + 1).wait_recv()

    for piece in range(PIECES):
        sends(0, piece, lambda copy: copy.start())

    for d in range(1, cols):
        other = lax.rem(c + cols - d, cols)
        remote(
            col_part(c), col_all.at[other, r], col_sent.at[d], col_got.at[d], (r, other)
        ).wait_recv()
    own_col.wait()

    def to_chip(d):
        other = 2 * lax.rem(chip + d, chips) + core
        return remote(
            col_all.at[:, r], col_all.at[:, r], chip_sent.at[d], chip_got.at[d], (other, c)
        )

    def from_chip(d):
        other = 2 * lax.rem(chip + chips - d, chips) + core
        return remote(
            col_all.at[:, other], col_all.at[:, other],
            chip_sent.at[d], chip_got.at[d], (other, c),
        )

    def to_twin(d):
        source = 2 * lax.rem(chip + chips - d, chips) + core
        return remote(
            col_all.at[:, source], col_all.at[:, source],
            pair_sent.at[d], pair_got.at[d], (twin, c),
        )

    def from_twin(d):
        source = 2 * lax.rem(chip + chips - d, chips) + 1 - core
        return remote(
            col_all.at[:, source], col_all.at[:, source],
            pair_sent.at[d], pair_got.at[d], (twin, c),
        )

    for d in range(1, chips):
        to_chip(d).start()
    to_twin(0).start()

    for step in range(cols - 2):
        for piece in range(PIECES):
            receives(step, piece)
            sends(step + 1, piece, lambda copy: copy.start())
    for d in range(1, chips):
        from_chip(d).wait_recv()
        to_twin(d).start()
    for piece in range(PIECES):
        receives(cols - 2, piece)
    for d in range(chips):
        from_twin(d).wait_recv()
    for copy in col_first + row_first:
        copy.wait_send()
    for step in range(cols - 1):
        for piece in range(PIECES):
            sends(step, piece, lambda copy: copy.wait_send())
    for d in range(1, chips):
        to_chip(d).wait_send()
    for d in range(chips):
        to_twin(d).wait_send()


def pairs_kernel(scaling, per, *refs):
    *views, out, held, sems = refs
    step = pl.program_id(0)
    last = pl.num_programs(0) - 1
    slot = lax.rem(step, 2)
    group, _, width = views[0].shape
    windows = len(views) // (1 + per) * group
    side = group * BINS
    into = lax.broadcasted_iota(jnp.int32, (side, side), 0)
    source = lax.broadcasted_iota(jnp.int32, (side, side), 1)
    swap = (into % group == source // BINS) & (into // group == source % BINS)
    swap = swap.astype(jnp.float32).astype(jnp.bfloat16)

    regrouped = []
    for part in range(2):
        bins = slice(part * BINS, (part + 1) * BINS)
        for first in range(0, len(views), 1 + per):
            pieces = [
                view[:, bins, :].reshape(side, width) for view in views[first : first + 1 + per]
            ]
            regrouped.append(
                jnp.dot(
                    swap, jnp.concatenate(pieces, axis=1), preferred_element_type=jnp.float32
                ).astype(jnp.bfloat16)
            )
    half = len(regrouped) // 2
    wide = per * width
    together = max(1, 256 // (2 * windows))
    depth = together * 2 * windows
    owner = lax.broadcasted_iota(jnp.int32, (width, depth), 1) // (2 * windows)
    groups = BINS // together

    def copies(at_step, at_slot):
        return [
            pltpu.make_async_copy(
                held.at[at_slot, part, pl.ds(g * together, together)],
                out.at[part, pl.ds(at_step * BINS + g * together, together)],
                sems.at[at_slot, part, g],
            )
            for g in range(groups)
            for part in range(2)
        ]

    @pl.when(step >= 2)
    def _():
        for copy in copies(step - 2, slot):
            copy.wait()

    outgoing = copies(step, slot)
    masks = [(owner == j).astype(jnp.float32).astype(jnp.bfloat16) for j in range(together)]
    for first in range(0, BINS, together):
        both, turned = [], []
        for bin_ in range(first, first + together):
            lines = slice(bin_ * group, (bin_ + 1) * group)
            both += [block[lines] for block in regrouped]
            turned += [-block[lines, 0:width] for block in regrouped[half:]]
            turned += [block[lines, 0:width] for block in regrouped[:half]]
        both = jnp.concatenate(both, axis=0)
        sides = [both[:, 0:width].T, jnp.concatenate(turned, axis=0).T]
        if together > 1:
            sides = [side * mask for mask in masks for side in sides]
        result = jnp.dot(
            jnp.concatenate(sides, axis=0), both[:, width:], preferred_element_type=jnp.float32
        )
        for j in range(together):
            for part in range(2):
                top = (2 * j + part) * width
                held[slot, part, first + j] = (result[top : top + width] * scaling).astype(
                    jnp.bfloat16
                )
        for part in range(2):
            outgoing[first // together * 2 + part].start()

    @pl.when(step == last)
    def _():
        for copy in copies(step - 1, 1 - slot) + outgoing:
            copy.wait()


def body(rows, cols, waveform, valid_mask, band_starts, station_map):
    _, stations, length = waveform.shape
    bands = band_starts.shape[0]
    double_bins = 2 * BINS * bands
    half = double_bins // 2
    width = stations // rows
    per = rows // cols
    windows = rows * cols
    steps = length // CHUNK
    whole = lambda shape: pl.BlockSpec(shape, lambda i: (0,) * len(shape))
    tables = phase_tables(band_starts, length)
    white = pl.pallas_call(
        functools.partial(spectra_kernel, length),
        grid=(steps,),
        out_shape=jax.ShapeDtypeStruct((rows, double_bins, width), jnp.bfloat16),
        in_specs=[
            pl.BlockSpec((1, stations // VIEWS, CHUNK), lambda i, view=view: (0, view, i))
            for view in range(VIEWS)
        ]
        + [
            whole((2, half, 128)),
            whole((2, half, 128)),
            whole((1, stations)),
            whole((1, stations)),
        ],
        out_specs=whole((rows, double_bins, width)),
        scratch_shapes=[
            pltpu.VMEM((stations, pl.cdiv(double_bins, 128) * 128), jnp.float32),
            pltpu.VMEM((double_bins, stations), jnp.float32),
            pltpu.VMEM((stations, 128), jnp.float32),
            pltpu.VMEM((double_bins, stations), jnp.bfloat16),
            pltpu.VMEM((half, CHUNK), jnp.float32),
            pltpu.VMEM((half, CHUNK), jnp.float32),
        ],
        compiler_params=pltpu.CompilerParams(vmem_limit_bytes=VMEM_BYTES),
        name="spectra",
    )(*[waveform] * VIEWS, *tables, valid_mask, station_map[None, :])

    dma = pltpu.SemaphoreType.DMA
    chips = rows // 2
    row_all, col_all = pl.pallas_call(
        functools.partial(exchange_kernel, rows, cols),
        out_shape=[
            jax.ShapeDtypeStruct((cols, rows, double_bins, width), jnp.bfloat16),
            jax.ShapeDtypeStruct((cols, rows, per, double_bins, width), jnp.bfloat16),
        ],
        in_specs=[pl.BlockSpec(memory_space=pl.ANY)],
        out_specs=[pl.BlockSpec(memory_space=pl.ANY)] * 2,
        scratch_shapes=[dma((2,)), dma((rows,)), dma((rows,)), dma((cols,)), dma((cols,))]
        + [dma((cols, PIECES))] * 4
        + [dma((chips,))] * 4,
        compiler_params=pltpu.CompilerParams(collective_id=0, has_side_effects=True, vmem_limit_bytes=VMEM_BYTES
        ),
        name="exchange",
    )(white)
    row_all = row_all.reshape(windows, double_bins, width)
    col_all = col_all.reshape(windows, per, double_bins, width)

    depth = 2 * BINS
    return pl.pallas_call(
        functools.partial(pairs_kernel, float(windows) ** (-0.5), per),
        grid=(bands,),
        out_shape=jax.ShapeDtypeStruct((2, half, width, per * width), jnp.bfloat16),
        in_specs=[
            spec
            for g in range(windows // GROUP)
            for spec in [pl.BlockSpec((GROUP, depth, width), lambda b, g=g: (g, b, 0))]
            + [
                pl.BlockSpec((GROUP, None, depth, width), lambda b, g=g, p=p: (g, p, b, 0))
                for p in range(per)
            ]
        ],
        out_specs=pl.BlockSpec(memory_space=pl.ANY),
        scratch_shapes=[
            pltpu.VMEM((2, 2, BINS, width, per * width), jnp.bfloat16),
            pltpu.SemaphoreType.DMA((2, 2, BINS)),
        ],
        compiler_params=pltpu.CompilerParams(vmem_limit_bytes=VMEM_BYTES),
        name="pairs",
    )(*([row_all] + [col_all] * per) * (windows // GROUP))


def solution(mesh):
    placed = (P(("row", "col"), None, None), P(("row", "col"), None), P(), P())
    return jax.shard_map(
        functools.partial(body, mesh.shape["row"], mesh.shape["col"]),
        mesh=mesh, in_specs=placed, out_specs=P(None, None, "row", "col"), check_vma=False,
    )
```

```python
import functools
import math

import jax
import jax.numpy as jnp
from jax import lax
from jax.experimental import pallas as pl
from jax.experimental.pallas import tpu as pltpu
from jax.sharding import PartitionSpec as P

BINS = 16
CHUNK = 1024
PIECES = 4
VIEWS = 4
VMEM_BYTES = 60 * 1024 * 1024
MESH = pl.DeviceIdType.MESH


def phase_tables(band_starts, length):
    frequency = (band_starts[:, None] + jnp.arange(BINS, dtype=jnp.int32)[None, :]).reshape(-1)
    samples = jnp.arange(128, dtype=jnp.int32)
    samples = jnp.stack([samples, samples * 128])
    phase = frequency[None, :, None] * samples[:, None, :] % length
    angles = phase.astype(jnp.float32) * jnp.float32(2.0 * math.pi / length)
    return jnp.cos(angles), jnp.sin(angles)


def spectra_kernel(
    length, *refs
):
    waves, refs = refs[:VIEWS], refs[VIEWS:]
    cosines, sines, mask, order, out, acc, squares, white, fine_cos, fine_sin = refs
    step = pl.program_id(0)
    each = waves[0].shape[1]
    stations = each * VIEWS
    double_bins = acc.shape[0]
    bands = double_bins // (2 * BINS)

    @pl.when(step == 0)
    def _():
        acc[...] = jnp.zeros_like(acc)
        squares[...] = jnp.zeros_like(squares)
        for tile in range(CHUNK // 128):
            tile_cos = cosines[1, :, tile : tile + 1]
            tile_sin = sines[1, :, tile : tile + 1]
            lanes = slice(tile * 128, (tile + 1) * 128)
            fine_cos[:, lanes] = tile_cos * cosines[0] - tile_sin * sines[0]
            fine_sin[:, lanes] = tile_sin * cosines[0] + tile_cos * sines[0]

    scale = length ** (-0.5)
    here = lax.broadcasted_iota(jnp.int32, cosines.shape[1:], 1) == step * (CHUNK // 128)
    first_cos = scale * jnp.sum(jnp.where(here, cosines[1], 0.0), axis=1, keepdims=True)
    first_sin = scale * jnp.sum(jnp.where(here, sines[1], 0.0), axis=1, keepdims=True)
    real = (first_cos * fine_cos[...] - first_sin * fine_sin[...]).astype(jnp.bfloat16)
    imag = (-(first_sin * fine_cos[...]) - first_cos * fine_sin[...]).astype(jnp.bfloat16)
    table = jnp.concatenate(
        [real.reshape(bands, BINS, CHUNK), imag.reshape(bands, BINS, CHUNK)], axis=1
    ).reshape(double_bins, CHUNK)
    for view, wave in enumerate(waves):
        base = view * each
        product = lax.dot_general(
            jnp.concatenate([table, wave[0]], axis=0),
            wave[0],
            (((1,), (1,)), ((), ())),
            preferred_element_type=jnp.float32,
        )
        acc[:, base : base + each] += product[0:double_bins]
        squares[view] += product[double_bins:]

    @pl.when(step == pl.num_programs(0) - 1)
    def _():
        diagonal = lax.broadcasted_iota(jnp.int32, (each, each), 0) == lax.broadcasted_iota(
            jnp.int32, (each, each), 1
        )
        sums = jnp.concatenate(
            [
                jnp.sum(jnp.where(diagonal, squares[view], 0.0), axis=0, keepdims=True)
                for view in range(VIEWS)
            ],
            axis=1,
        )
        inverse = 1.0 / jnp.sqrt(sums / length + 1e-06)
        valid = mask[...].astype(jnp.float32)
        for band in range(bands):
            top = band * 2 * BINS
            re = acc[top : top + BINS, :] * inverse
            im = acc[top + BINS : top + 2 * BINS, :] * inverse
            power = re * re + im * im
            mean = jnp.mean(power, axis=0, keepdims=True)
            factor = valid / jnp.sqrt(power + mean + 0.1)
            white[top : top + BINS, :] = (re * factor).astype(jnp.bfloat16)
            white[top + BINS : top + 2 * BINS, :] = (im * factor).astype(jnp.bfloat16)
        blocks, _, width = out.shape
        group = 256
        for start in range(0, stations, group):
            source = lax.broadcasted_iota(jnp.int32, (stations, group), 0)
            pick = (source == order[0:1, start : start + group]).astype(jnp.float32)
            placed = jnp.dot(
                white[...], pick.astype(jnp.bfloat16), preferred_element_type=jnp.float32
            ).astype(jnp.bfloat16)
            for inner in range(group // width):
                out[start // width + inner] = placed[:, inner * width : (inner + 1) * width]


def exchange_kernel(
    rows, cols, white, row_all, col_all,
    local_sem, row_sent, row_got, col_sent, col_got,
    right_sent, right_got, left_sent, left_got, chip_sent, chip_got, pair_sent, pair_got,
):
    r = lax.axis_index("row")
    c = lax.axis_index("col")
    chips = rows // 2
    core = lax.rem(r, 2)
    chip = r // 2
    twin = r + 1 - 2 * core
    per = rows // cols

    barrier = pltpu.get_barrier_semaphore()
    for d in range(1, rows):
        pl.semaphore_signal(
            barrier, inc=1, device_id=(lax.rem(r + d, rows), c), device_id_type=MESH
        )
    for d in range(1, cols):
        pl.semaphore_signal(
            barrier, inc=1, device_id=(r, lax.rem(c + d, cols)), device_id_type=MESH
        )
    pl.semaphore_wait(barrier, rows - 1 + cols - 1)

    def remote(src, dst, sent, got, target):
        return pltpu.make_async_remote_copy(
            src_ref=src, dst_ref=dst, send_sem=sent, recv_sem=got,
            device_id=target, device_id_type=MESH,
        )

    def col_part(block):
        return white.at[pl.ds(block * per, per)]

    col_first = []
    for d in range(1, cols):
        other = lax.rem(c + d, cols)
        col_first.append(
            remote(col_part(other), col_all.at[c, r], col_sent.at[d], col_got.at[d], (r, other))
        )
        col_first[-1].start()
    row_first = []
    for d in range(1, rows):
        other = lax.rem(r + d, rows)
        row_first.append(
            remote(white.at[other], row_all.at[c, r], row_sent.at[d], row_got.at[d], (other, c))
        )
        row_first[-1].start()
    own_row = pltpu.make_async_copy(white.at[r], row_all.at[c, r], local_sem.at[0])
    own_row.start()
    own_col = pltpu.make_async_copy(col_part(c), col_all.at[c, r], local_sem.at[1])
    own_col.start()

    for d in range(1, rows):
        other = lax.rem(r + rows - d, rows)
        remote(
            white.at[r], row_all.at[c, other], row_sent.at[d], row_got.at[d], (other, c)
        ).wait_recv()
    own_row.wait()

    def piece_of(block, piece):
        return row_all.at[block, pl.ds(piece * (rows // PIECES), rows // PIECES)]

    def passing(block, piece, sent, got, step, target):
        ref = piece_of(block, piece)
        return remote(ref, ref, sent.at[step, piece], got.at[step, piece], (r, target))

    def sends(step, piece, act):
        @pl.when((c + 1 < cols) & (c - step >= 0))
        def _():
            act(passing(c - step, piece, right_sent, right_got, step, c + 1))

        @pl.when((c - 1 >= 0) & (c + step < cols))
        def _():
            act(passing(c + step, piece, left_sent, left_got, step, c - 1))

    def receives(step, piece):
        @pl.when(c - 1 - step >= 0)
        def _():
            passing(c - 1 - step, piece, right_sent, right_got, step, c - 1).wait_recv()

        @pl.when(c + 1 + step < cols)
        def _():
            passing(c + 1 + step, piece, left_sent, left_got, step, c + 1).wait_recv()

    for piece in range(PIECES):
        sends(0, piece, lambda copy: copy.start())

    for d in range(1, cols):
        other = lax.rem(c + cols - d, cols)
        remote(
            col_part(c), col_all.at[other, r], col_sent.at[d], col_got.at[d], (r, other)
        ).wait_recv()
    own_col.wait()

    def to_chip(d):
        other = 2 * lax.rem(chip + d, chips) + core
        return remote(
            col_all.at[:, r], col_all.at[:, r], chip_sent.at[d], chip_got.at[d], (other, c)
        )

    def from_chip(d):
        other = 2 * lax.rem(chip + chips - d, chips) + core
        return remote(
            col_all.at[:, other], col_all.at[:, other],
            chip_sent.at[d], chip_got.at[d], (other, c),
        )

    def to_twin(d):
        source = 2 * lax.rem(chip + chips - d, chips) + core
        return remote(
            col_all.at[:, source], col_all.at[:, source],
            pair_sent.at[d], pair_got.at[d], (twin, c),
        )

    def from_twin(d):
        source = 2 * lax.rem(chip + chips - d, chips) + 1 - core
        return remote(
            col_all.at[:, source], col_all.at[:, source],
            pair_sent.at[d], pair_got.at[d], (twin, c),
        )

    for d in range(1, chips):
        to_chip(d).start()
    to_twin(0).start()

    for step in range(cols - 2):
        for piece in range(PIECES):
            receives(step, piece)
            sends(step + 1, piece, lambda copy: copy.start())
    for d in range(1, chips):
        from_chip(d).wait_recv()
        to_twin(d).start()
    for piece in range(PIECES):
        receives(cols - 2, piece)
    for d in range(chips):
        from_twin(d).wait_recv()
    for copy in col_first + row_first:
        copy.wait_send()
    for step in range(cols - 1):
        for piece in range(PIECES):
            sends(step, piece, lambda copy: copy.wait_send())
    for d in range(1, chips):
        to_chip(d).wait_send()
    for d in range(chips):
        to_twin(d).wait_send()


def pairs_kernel(scaling, row_block, col_block, out, held, sems):
    step = pl.program_id(0)
    last = pl.num_programs(0) - 1
    slot = lax.rem(step, 2)
    windows, _, width = row_block.shape
    per = col_block.shape[1]
    group = 16
    side = group * BINS
    into = lax.broadcasted_iota(jnp.int32, (side, side), 0)
    source = lax.broadcasted_iota(jnp.int32, (side, side), 1)
    swap = (into % group == source // BINS) & (into // group == source % BINS)
    swap = swap.astype(jnp.float32).astype(jnp.bfloat16)

    regrouped = []
    for part in range(2):
        bins = slice(part * BINS, (part + 1) * BINS)
        for first in range(0, windows, group):
            pieces = [row_block[first : first + group, bins, :].reshape(side, width)]
            for block in range(per):
                pieces.append(col_block[first : first + group, block, bins, :].reshape(side, width))
            regrouped.append(
                jnp.dot(
                    swap, jnp.concatenate(pieces, axis=1), preferred_element_type=jnp.float32
                ).astype(jnp.bfloat16)
            )
    half = len(regrouped) // 2
    wide = per * width
    together = max(1, 256 // (2 * windows))
    depth = together * 2 * windows
    owner = lax.broadcasted_iota(jnp.int32, (width, depth), 1) // (2 * windows)
    groups = BINS // together

    def copies(at_step, at_slot):
        return [
            pltpu.make_async_copy(
                held.at[at_slot, part, pl.ds(g * together, together)],
                out.at[part, pl.ds(at_step * BINS + g * together, together)],
                sems.at[at_slot, part, g],
            )
            for g in range(groups)
            for part in range(2)
        ]

    @pl.when(step >= 2)
    def _():
        for copy in copies(step - 2, slot):
            copy.wait()

    outgoing = copies(step, slot)
    masks = [(owner == j).astype(jnp.float32).astype(jnp.bfloat16) for j in range(together)]
    for first in range(0, BINS, together):
        both, turned = [], []
        for bin_ in range(first, first + together):
            lines = slice(bin_ * group, (bin_ + 1) * group)
            both += [block[lines] for block in regrouped]
            turned += [-block[lines, 0:width] for block in regrouped[half:]]
            turned += [block[lines, 0:width] for block in regrouped[:half]]
        both = jnp.concatenate(both, axis=0)
        sides = [both[:, 0:width].T, jnp.concatenate(turned, axis=0).T]
        if together > 1:
            sides = [side * mask for mask in masks for side in sides]
        result = jnp.dot(
            jnp.concatenate(sides, axis=0), both[:, width:], preferred_element_type=jnp.float32
        )
        for j in range(together):
            for part in range(2):
                top = (2 * j + part) * width
                held[slot, part, first + j] = (result[top : top + width] * scaling).astype(
                    jnp.bfloat16
                )
        for part in range(2):
            outgoing[first // together * 2 + part].start()

    @pl.when(step == last)
    def _():
        for copy in copies(step - 1, 1 - slot) + outgoing:
            copy.wait()


def body(rows, cols, waveform, valid_mask, band_starts, station_map):
    _, stations, length = waveform.shape
    bands = band_starts.shape[0]
    double_bins = 2 * BINS * bands
    half = double_bins // 2
    width = stations // rows
    per = rows // cols
    windows = rows * cols
    steps = length // CHUNK
    whole = lambda shape: pl.BlockSpec(shape, lambda i: (0,) * len(shape))
    tables = phase_tables(band_starts, length)
    white = pl.pallas_call(
        functools.partial(spectra_kernel, length),
        grid=(steps,),
        out_shape=jax.ShapeDtypeStruct((rows, double_bins, width), jnp.bfloat16),
        in_specs=[
            pl.BlockSpec((1, stations // VIEWS, CHUNK), lambda i, view=view: (0, view, i))
            for view in range(VIEWS)
        ]
        + [
            whole((2, half, 128)),
            whole((2, half, 128)),
            whole((1, stations)),
            whole((1, stations)),
        ],
        out_specs=whole((rows, double_bins, width)),
        scratch_shapes=[
            pltpu.VMEM((double_bins, stations), jnp.float32),
            pltpu.VMEM((VIEWS, stations // VIEWS, stations // VIEWS), jnp.float32),
            pltpu.VMEM((double_bins, stations), jnp.bfloat16),
            pltpu.VMEM((half, CHUNK), jnp.float32),
            pltpu.VMEM((half, CHUNK), jnp.float32),
        ],
        compiler_params=pltpu.CompilerParams(vmem_limit_bytes=VMEM_BYTES),
        name="spectra",
    )(*[waveform] * VIEWS, *tables, valid_mask, station_map[None, :])

    dma = pltpu.SemaphoreType.DMA
    chips = rows // 2
    row_all, col_all = pl.pallas_call(
        functools.partial(exchange_kernel, rows, cols),
        out_shape=[
            jax.ShapeDtypeStruct((cols, rows, double_bins, width), jnp.bfloat16),
            jax.ShapeDtypeStruct((cols, rows, per, double_bins, width), jnp.bfloat16),
        ],
        in_specs=[pl.BlockSpec(memory_space=pl.ANY)],
        out_specs=[pl.BlockSpec(memory_space=pl.ANY)] * 2,
        scratch_shapes=[dma((2,)), dma((rows,)), dma((rows,)), dma((cols,)), dma((cols,))]
        + [dma((cols, PIECES))] * 4
        + [dma((chips,))] * 4,
        compiler_params=pltpu.CompilerParams(collective_id=0, has_side_effects=True, vmem_limit_bytes=VMEM_BYTES
        ),
        name="exchange",
    )(white)
    row_all = row_all.reshape(windows, double_bins, width)
    col_all = col_all.reshape(windows, per, double_bins, width)

    depth = 2 * BINS
    return pl.pallas_call(
        functools.partial(pairs_kernel, float(windows) ** (-0.5)),
        grid=(bands,),
        out_shape=jax.ShapeDtypeStruct((2, half, width, per * width), jnp.bfloat16),
        in_specs=[
            pl.BlockSpec((windows, depth, width), lambda b: (0, b, 0)),
            pl.BlockSpec((windows, per, depth, width), lambda b: (0, 0, b, 0)),
        ],
        out_specs=pl.BlockSpec(memory_space=pl.ANY),
        scratch_shapes=[
            pltpu.VMEM((2, 2, BINS, width, per * width), jnp.bfloat16),
            pltpu.SemaphoreType.DMA((2, 2, BINS)),
        ],
        compiler_params=pltpu.CompilerParams(vmem_limit_bytes=VMEM_BYTES),
        name="pairs",
    )(row_all, col_all)


def solution(mesh):
    placed = (P(("row", "col"), None, None), P(("row", "col"), None), P(), P())
    return jax.shard_map(
        functools.partial(body, mesh.shape["row"], mesh.shape["col"]),
        mesh=mesh, in_specs=placed, out_specs=P(None, None, "row", "col"), check_vma=False,
    )
```

```python
import functools
import math

import jax
import jax.numpy as jnp
from jax import lax
from jax.experimental import pallas as pl
from jax.experimental.pallas import tpu as pltpu
from jax.sharding import PartitionSpec as P

BINS = 16
CHUNK = 2048
PIECES = 2
VIEWS = 4
VMEM_BYTES = 60 * 1024 * 1024
MESH = pl.DeviceIdType.MESH


def phase_tables(band_starts, length):
    frequency = (band_starts[:, None] + jnp.arange(BINS, dtype=jnp.int32)[None, :]).reshape(-1)
    samples = jnp.arange(128, dtype=jnp.int32)
    samples = jnp.stack([samples, samples * 128])
    phase = frequency[None, :, None] * samples[:, None, :] % length
    angles = phase.astype(jnp.float32) * jnp.float32(2.0 * math.pi / length)
    return jnp.cos(angles), jnp.sin(angles)


def spectra_kernel(
    length, *refs
):
    waves, refs = refs[:VIEWS], refs[VIEWS:]
    cosines, sines, mask, order, out, acc, squares, white, fine_cos, fine_sin = refs
    step = pl.program_id(0)
    each = waves[0].shape[1]
    stations = each * VIEWS
    double_bins = acc.shape[0]
    bands = double_bins // (2 * BINS)

    @pl.when(step == 0)
    def _():
        acc[...] = jnp.zeros_like(acc)
        squares[...] = jnp.zeros_like(squares)
        for tile in range(CHUNK // 128):
            tile_cos = cosines[1, :, tile : tile + 1]
            tile_sin = sines[1, :, tile : tile + 1]
            lanes = slice(tile * 128, (tile + 1) * 128)
            fine_cos[:, lanes] = tile_cos * cosines[0] - tile_sin * sines[0]
            fine_sin[:, lanes] = tile_sin * cosines[0] + tile_cos * sines[0]

    scale = length ** (-0.5)
    here = lax.broadcasted_iota(jnp.int32, cosines.shape[1:], 1) == step * (CHUNK // 128)
    first_cos = scale * jnp.sum(jnp.where(here, cosines[1], 0.0), axis=1, keepdims=True)
    first_sin = scale * jnp.sum(jnp.where(here, sines[1], 0.0), axis=1, keepdims=True)
    real = (first_cos * fine_cos[...] - first_sin * fine_sin[...]).astype(jnp.bfloat16)
    imag = (-(first_sin * fine_cos[...]) - first_cos * fine_sin[...]).astype(jnp.bfloat16)
    table = jnp.concatenate(
        [real.reshape(bands, BINS, CHUNK), imag.reshape(bands, BINS, CHUNK)], axis=1
    ).reshape(double_bins, CHUNK)
    for view, wave in enumerate(waves):
        base = view * each
        acc[:, base : base + each] += lax.dot_general(
            table, wave[0], (((1,), (1,)), ((), ())), preferred_element_type=jnp.float32
        )
        for top in range(0, each, 64):
            total = squares[base + top : base + top + 64, :]
            for tile in range(CHUNK // 128):
                part = wave[0, top : top + 64, tile * 128 : (tile + 1) * 128].astype(jnp.float32)
                total = total + part * part
            squares[base + top : base + top + 64, :] = total

    @pl.when(step == pl.num_programs(0) - 1)
    def _():
        ones = jnp.ones((8, 128), jnp.float32)
        sums = lax.dot_general(
            ones,
            squares[...],
            (((1,), (1,)), ((), ())),
            precision=lax.Precision.HIGHEST,
            preferred_element_type=jnp.float32,
        )[0:1]
        inverse = 1.0 / jnp.sqrt(sums / length + 1e-06)
        valid = mask[...].astype(jnp.float32)
        for band in range(bands):
            top = band * 2 * BINS
            re = acc[top : top + BINS, :] * inverse
            im = acc[top + BINS : top + 2 * BINS, :] * inverse
            power = re * re + im * im
            mean = jnp.mean(power, axis=0, keepdims=True)
            factor = valid / jnp.sqrt(power + mean + 0.1)
            white[top : top + BINS, :] = (re * factor).astype(jnp.bfloat16)
            white[top + BINS : top + 2 * BINS, :] = (im * factor).astype(jnp.bfloat16)
        blocks, _, width = out.shape
        group = 256
        for start in range(0, stations, group):
            source = lax.broadcasted_iota(jnp.int32, (stations, group), 0)
            pick = (source == order[0:1, start : start + group]).astype(jnp.float32)
            placed = jnp.dot(
                white[...], pick.astype(jnp.bfloat16), preferred_element_type=jnp.float32
            ).astype(jnp.bfloat16)
            for inner in range(group // width):
                out[start // width + inner] = placed[:, inner * width : (inner + 1) * width]


def exchange_kernel(
    rows, cols, white, row_all, col_all,
    local_sem, row_sent, row_got, col_sent, col_got,
    right_sent, right_got, left_sent, left_got, chip_sent, chip_got, pair_sent, pair_got,
):
    r = lax.axis_index("row")
    c = lax.axis_index("col")
    chips = rows // 2
    core = lax.rem(r, 2)
    chip = r // 2
    twin = r + 1 - 2 * core
    per = rows // cols

    barrier = pltpu.get_barrier_semaphore()
    for d in range(1, rows):
        pl.semaphore_signal(
            barrier, inc=1, device_id=(lax.rem(r + d, rows), c), device_id_type=MESH
        )
    for d in range(1, cols):
        pl.semaphore_signal(
            barrier, inc=1, device_id=(r, lax.rem(c + d, cols)), device_id_type=MESH
        )
    pl.semaphore_wait(barrier, rows - 1 + cols - 1)

    def remote(src, dst, sent, got, target):
        return pltpu.make_async_remote_copy(
            src_ref=src, dst_ref=dst, send_sem=sent, recv_sem=got,
            device_id=target, device_id_type=MESH,
        )

    def col_part(block):
        return white.at[pl.ds(block * per, per)]

    col_first = []
    for d in range(1, cols):
        other = lax.rem(c + d, cols)
        col_first.append(
            remote(col_part(other), col_all.at[c, r], col_sent.at[d], col_got.at[d], (r, other))
        )
        col_first[-1].start()
    row_first = []
    for d in range(1, rows):
        other = lax.rem(r + d, rows)
        row_first.append(
            remote(white.at[other], row_all.at[c, r], row_sent.at[d], row_got.at[d], (other, c))
        )
        row_first[-1].start()
    own_row = pltpu.make_async_copy(white.at[r], row_all.at[c, r], local_sem.at[0])
    own_row.start()
    own_col = pltpu.make_async_copy(col_part(c), col_all.at[c, r], local_sem.at[1])
    own_col.start()

    for d in range(1, rows):
        other = lax.rem(r + rows - d, rows)
        remote(
            white.at[r], row_all.at[c, other], row_sent.at[d], row_got.at[d], (other, c)
        ).wait_recv()
    own_row.wait()

    def piece_of(block, piece):
        return row_all.at[block, pl.ds(piece * (rows // PIECES), rows // PIECES)]

    def passing(block, piece, sent, got, step, target):
        ref = piece_of(block, piece)
        return remote(ref, ref, sent.at[step, piece], got.at[step, piece], (r, target))

    def sends(step, piece, act):
        @pl.when((c + 1 < cols) & (c - step >= 0))
        def _():
            act(passing(c - step, piece, right_sent, right_got, step, c + 1))

        @pl.when((c - 1 >= 0) & (c + step < cols))
        def _():
            act(passing(c + step, piece, left_sent, left_got, step, c - 1))

    def receives(step, piece):
        @pl.when(c - 1 - step >= 0)
        def _():
            passing(c - 1 - step, piece, right_sent, right_got, step, c - 1).wait_recv()

        @pl.when(c + 1 + step < cols)
        def _():
            passing(c + 1 + step, piece, left_sent, left_got, step, c + 1).wait_recv()

    for piece in range(PIECES):
        sends(0, piece, lambda copy: copy.start())

    for d in range(1, cols):
        other = lax.rem(c + cols - d, cols)
        remote(
            col_part(c), col_all.at[other, r], col_sent.at[d], col_got.at[d], (r, other)
        ).wait_recv()
    own_col.wait()

    def to_chip(d):
        other = 2 * lax.rem(chip + d, chips) + core
        return remote(
            col_all.at[:, r], col_all.at[:, r], chip_sent.at[d], chip_got.at[d], (other, c)
        )

    def from_chip(d):
        other = 2 * lax.rem(chip + chips - d, chips) + core
        return remote(
            col_all.at[:, other], col_all.at[:, other],
            chip_sent.at[d], chip_got.at[d], (other, c),
        )

    def to_twin(d):
        source = 2 * lax.rem(chip + chips - d, chips) + core
        return remote(
            col_all.at[:, source], col_all.at[:, source],
            pair_sent.at[d], pair_got.at[d], (twin, c),
        )

    def from_twin(d):
        source = 2 * lax.rem(chip + chips - d, chips) + 1 - core
        return remote(
            col_all.at[:, source], col_all.at[:, source],
            pair_sent.at[d], pair_got.at[d], (twin, c),
        )

    for d in range(1, chips):
        to_chip(d).start()
    to_twin(0).start()

    for step in range(cols - 2):
        for piece in range(PIECES):
            receives(step, piece)
            sends(step + 1, piece, lambda copy: copy.start())
    for d in range(1, chips):
        from_chip(d).wait_recv()
        to_twin(d).start()
    for piece in range(PIECES):
        receives(cols - 2, piece)
    for d in range(chips):
        from_twin(d).wait_recv()
    for copy in col_first + row_first:
        copy.wait_send()
    for step in range(cols - 1):
        for piece in range(PIECES):
            sends(step, piece, lambda copy: copy.wait_send())
    for d in range(1, chips):
        to_chip(d).wait_send()
    for d in range(chips):
        to_twin(d).wait_send()


def pairs_kernel(scaling, row_block, col_block, out, held, sems):
    step = pl.program_id(0)
    last = pl.num_programs(0) - 1
    slot = lax.rem(step, 2)
    windows, _, width = row_block.shape
    per = col_block.shape[1]
    group = 16
    side = group * BINS
    into = lax.broadcasted_iota(jnp.int32, (side, side), 0)
    source = lax.broadcasted_iota(jnp.int32, (side, side), 1)
    swap = (into % group == source // BINS) & (into // group == source % BINS)
    swap = swap.astype(jnp.float32).astype(jnp.bfloat16)

    regrouped = []
    for part in range(2):
        bins = slice(part * BINS, (part + 1) * BINS)
        for first in range(0, windows, group):
            pieces = [row_block[first : first + group, bins, :].reshape(side, width)]
            for block in range(per):
                pieces.append(col_block[first : first + group, block, bins, :].reshape(side, width))
            regrouped.append(
                jnp.dot(
                    swap, jnp.concatenate(pieces, axis=1), preferred_element_type=jnp.float32
                ).astype(jnp.bfloat16)
            )
    half = len(regrouped) // 2
    wide = per * width
    together = max(1, 256 // (2 * windows))
    depth = together * 2 * windows
    owner = lax.broadcasted_iota(jnp.int32, (width, depth), 1) // (2 * windows)
    groups = BINS // together

    def copies(at_step, at_slot):
        return [
            pltpu.make_async_copy(
                held.at[at_slot, part, pl.ds(g * together, together)],
                out.at[part, pl.ds(at_step * BINS + g * together, together)],
                sems.at[at_slot, part, g],
            )
            for g in range(groups)
            for part in range(2)
        ]

    @pl.when(step >= 2)
    def _():
        for copy in copies(step - 2, slot):
            copy.wait()

    outgoing = copies(step, slot)
    masks = [(owner == j).astype(jnp.float32).astype(jnp.bfloat16) for j in range(together)]
    for first in range(0, BINS, together):
        both, turned = [], []
        for bin_ in range(first, first + together):
            lines = slice(bin_ * group, (bin_ + 1) * group)
            both += [block[lines] for block in regrouped]
            turned += [-block[lines, 0:width] for block in regrouped[half:]]
            turned += [block[lines, 0:width] for block in regrouped[:half]]
        both = jnp.concatenate(both, axis=0)
        sides = [both[:, 0:width].T, jnp.concatenate(turned, axis=0).T]
        if together > 1:
            sides = [side * mask for mask in masks for side in sides]
        result = jnp.dot(
            jnp.concatenate(sides, axis=0), both[:, width:], preferred_element_type=jnp.float32
        )
        for j in range(together):
            for part in range(2):
                top = (2 * j + part) * width
                held[slot, part, first + j] = (result[top : top + width] * scaling).astype(
                    jnp.bfloat16
                )
        for part in range(2):
            outgoing[first // together * 2 + part].start()

    @pl.when(step == last)
    def _():
        for copy in copies(step - 1, 1 - slot) + outgoing:
            copy.wait()


def body(rows, cols, waveform, valid_mask, band_starts, station_map):
    _, stations, length = waveform.shape
    bands = band_starts.shape[0]
    double_bins = 2 * BINS * bands
    half = double_bins // 2
    width = stations // rows
    per = rows // cols
    windows = rows * cols
    steps = length // CHUNK
    whole = lambda shape: pl.BlockSpec(shape, lambda i: (0,) * len(shape))
    tables = phase_tables(band_starts, length)
    white = pl.pallas_call(
        functools.partial(spectra_kernel, length),
        grid=(steps,),
        out_shape=jax.ShapeDtypeStruct((rows, double_bins, width), jnp.bfloat16),
        in_specs=[
            pl.BlockSpec((1, stations // VIEWS, CHUNK), lambda i, view=view: (0, view, i))
            for view in range(VIEWS)
        ]
        + [
            whole((2, half, 128)),
            whole((2, half, 128)),
            whole((1, stations)),
            whole((1, stations)),
        ],
        out_specs=whole((rows, double_bins, width)),
        scratch_shapes=[
            pltpu.VMEM((double_bins, stations), jnp.float32),
            pltpu.VMEM((stations, 128), jnp.float32),
            pltpu.VMEM((double_bins, stations), jnp.bfloat16),
            pltpu.VMEM((half, CHUNK), jnp.float32),
            pltpu.VMEM((half, CHUNK), jnp.float32),
        ],
        compiler_params=pltpu.CompilerParams(vmem_limit_bytes=VMEM_BYTES),
        name="spectra",
    )(*[waveform] * VIEWS, *tables, valid_mask, station_map[None, :])

    dma = pltpu.SemaphoreType.DMA
    chips = rows // 2
    row_all, col_all = pl.pallas_call(
        functools.partial(exchange_kernel, rows, cols),
        out_shape=[
            jax.ShapeDtypeStruct((cols, rows, double_bins, width), jnp.bfloat16),
            jax.ShapeDtypeStruct((cols, rows, per, double_bins, width), jnp.bfloat16),
        ],
        in_specs=[pl.BlockSpec(memory_space=pl.ANY)],
        out_specs=[pl.BlockSpec(memory_space=pl.ANY)] * 2,
        scratch_shapes=[dma((2,)), dma((rows,)), dma((rows,)), dma((cols,)), dma((cols,))]
        + [dma((cols, PIECES))] * 4
        + [dma((chips,))] * 4,
        compiler_params=pltpu.CompilerParams(collective_id=0, has_side_effects=True, vmem_limit_bytes=VMEM_BYTES
        ),
        name="exchange",
    )(white)
    row_all = row_all.reshape(windows, double_bins, width)
    col_all = col_all.reshape(windows, per, double_bins, width)

    depth = 2 * BINS
    return pl.pallas_call(
        functools.partial(pairs_kernel, float(windows) ** (-0.5)),
        grid=(bands,),
        out_shape=jax.ShapeDtypeStruct((2, half, width, per * width), jnp.bfloat16),
        in_specs=[
            pl.BlockSpec((windows, depth, width), lambda b: (0, b, 0)),
            pl.BlockSpec((windows, per, depth, width), lambda b: (0, 0, b, 0)),
        ],
        out_specs=pl.BlockSpec(memory_space=pl.ANY),
        scratch_shapes=[
            pltpu.VMEM((2, 2, BINS, width, per * width), jnp.bfloat16),
            pltpu.SemaphoreType.DMA((2, 2, BINS)),
        ],
        compiler_params=pltpu.CompilerParams(vmem_limit_bytes=VMEM_BYTES),
        name="pairs",
    )(row_all, col_all)


def solution(mesh):
    placed = (P(("row", "col"), None, None), P(("row", "col"), None), P(), P())
    return jax.shard_map(
        functools.partial(body, mesh.shape["row"], mesh.shape["col"]),
        mesh=mesh, in_specs=placed, out_specs=P(None, None, "row", "col"), check_vma=False,
    )
```
